32 devices in a mesh: gx: 16 (over z, y, core), gy: 2 (over x).
Axes of the slice: x: 2, y: 2, z: 4, core: 2. Of those that a mesh axis runs over, the one named last changes fastest.
Arguments:
- input_one: float32 [32, 2, 64, 256], P(None, None, 'gx', 'gy'), may hold values from -6 to 6
- input_two: float32 [32, 2, 64, 256], P(None, None, 'gx', 'gy'), may hold values from -6 to 6
- input_three: float32 [32, 2, 64, 256], P(None, None, 'gx', 'gy'), may hold values from -6 to 6
- cotangent: float32 [32, 2, 64, 256], P(None, None, 'gx', 'gy'), may hold values from -6 to 6
- kernel_one: float32 [27, 32, 32], replicated, may hold values from -0.21875 to 0.21875
- kernel_two: float32 [27, 32, 32], replicated, may hold values from -0.21875 to 0.21875
- kernel_three: float32 [27, 32, 32], replicated, may hold values from -0.21875 to 0.21875
Outputs:
- grad_input: float32 [32, 2, 64, 256], P(None, None, 'gx', 'gy')
- grad_kernel_one: float32 [27, 32, 32], replicated
- grad_kernel_two: float32 [27, 32, 32], replicated
- grad_kernel_three: float32 [27, 32, 32], replicated
The draws below stay inside these ranges and needn't reach their ends.
All inputs are finite; a program needn't handle non-finite values.
Results may differ from the reference program's by a relative error of at most 0.00013.
Values sent between devices are 32-bit elements; how exact they have to be, the bound alone decides.
No kernel may reach another device: no remote copies, remote signals or barrier semaphores. Data moves between devices by JAX's collectives and lax.ppermute only.
A program may use at most 64 MiB of HBM per device.

```python
import math
import jax
import jax.numpy as jnp
from jax import lax

C = 32
NZ = 2
NX = 64
NY = 256


def shard_levels(own_key, extent, split, low, top_value):
    factor_of, own = 1.0, jax.random.fold_in(own_key, 6)
    for axis_at, blocks in split:
        heights = jnp.exp(jax.random.uniform(jax.random.fold_in(own, axis_at), (blocks,), jnp.float32, low / len(split), top_value / len(split)))
        factor_of = factor_of * jnp.repeat(heights, extent[axis_at] // blocks).reshape([-1 if axis == axis_at else 1 for axis in range(len(extent))])
    return factor_of


def normal_values(key, shape, spread, reach, shards=(), kind=jnp.bfloat16):
    entries = spread * jax.random.normal(key, shape, jnp.float32)
    if shards:
        entries = entries * shard_levels(key, shape, shards, -0.22, 0.18)
    return jnp.clip(entries, -reach, reach).astype(kind)


def setup_inputs(seed: int = 0) -> dict:
    key_list = jax.random.split(jax.random.key(seed), 8)
    return {
        "input_one": normal_values(key_list[0], (C, NZ, NX, NY), 1.0, 6.0, ((2, 16), (3, 2)), jnp.float32),
        "input_two": normal_values(key_list[1], (C, NZ, NX, NY), 1.0, 6.0, ((2, 16), (3, 2)), jnp.float32),
        "input_three": normal_values(key_list[2], (C, NZ, NX, NY), 1.0, 6.0, ((2, 16), (3, 2)), jnp.float32),
        "cotangent": normal_values(key_list[3], (C, NZ, NX, NY), 1.0, 6.0, ((2, 16), (3, 2)), jnp.float32),
        "kernel_one": normal_values(key_list[4], (27, C, C), (27 * C) ** -0.5, 0.21875, (), jnp.float32),
        "kernel_two": normal_values(key_list[5], (27, C, C), (27 * C) ** -0.5, 0.21875, (), jnp.float32),
        "kernel_three": normal_values(key_list[6], (27, C, C), (27 * C) ** -0.5, 0.21875, (), jnp.float32),
    }


inv_root_two = 0.7071067811865476
inv_root_two_pi = 0.3989422804014327

def gelu_slope(value):
    normal_cdf = 0.5 * (1.0 + jax.scipy.special.erf(value * inv_root_two))
    density = jnp.exp(-0.5 * value * value) * inv_root_two_pi
    return normal_cdf + value * density

def conv_taps(padded, kernel, depth, rows, cols):
    total = None
    for tap in range(27):
        a, b, c = (tap // 9, tap // 3 % 3, tap % 3)
        window = padded[:, a:a + depth, b:b + rows, c:c + cols]
        term = jnp.einsum('oi,izxy->ozxy', kernel[tap], window, precision=lax.Precision.HIGHEST)
        total = term if total is None else total + term
    return total

def back_taps(padded, kernel, depth, rows, cols):
    total = None
    for tap in range(27):
        a, b, c = (tap // 9, tap // 3 % 3, tap % 3)
        window = padded[:, 2 - a:2 - a + depth, 2 - b:2 - b + rows, 2 - c:2 - c + cols]
        term = jnp.einsum('oi,ozxy->izxy', kernel[tap], window, precision=lax.Precision.HIGHEST)
        total = term if total is None else total + term
    return total

def kernel_terms(padded, slope_grad, depth, rows, cols):
    parts = []
    for tap in range(27):
        a, b, c = (tap // 9, tap // 3 % 3, tap % 3)
        window = padded[:, a:a + depth, b:b + rows, c:c + cols]
        parts.append(jnp.einsum('ozxy,izxy->oi', slope_grad, window, precision=lax.Precision.HIGHEST))
    return jnp.stack(parts, axis=0)

def reference(input_one, input_two, input_three, cotangent, kernel_one, kernel_two, kernel_three):
    depth, rows, cols = (input_one.shape[1], input_one.shape[2], input_one.shape[3])
    factor = 1.0 / math.sqrt(depth * rows * cols)
    widths = ((0, 0), (1, 1), (1, 1), (1, 1))
    grad = cotangent
    results = []
    for field, kernel in ((input_three, kernel_three), (input_two, kernel_two), (input_one, kernel_one)):
        padded = jnp.pad(field, widths)
        pre = conv_taps(padded, kernel, depth, rows, cols)
        slope_grad = grad * gelu_slope(pre)
        results.append(kernel_terms(padded, slope_grad, depth, rows, cols) * factor)
        grad = back_taps(jnp.pad(slope_grad, widths), kernel, depth, rows, cols)
    return (grad, results[2], results[1], results[0])
```

```python
import functools
import math

import jax
import jax.numpy as jnp
from jax import lax
from jax.experimental import pallas as pl
from jax.experimental.pallas import tpu as pltpu
from jax.sharding import PartitionSpec as P

inv_root_two = 0.7071067811865476
inv_root_two_pi = 0.3989422804014327

LAYERS = 3
HALO = LAYERS + 1
SIDE = 2 * HALO
LANES = 128
F32 = jnp.float32
BF16 = jnp.bfloat16
NN = (((1,), (0,)), ((), ()))
NT = (((1,), (1,)), ((), ()))

WIDTHS = (HALO, HALO - 1, HALO - 1, HALO - 2)
STARTS = tuple(sum(WIDTHS[:f]) for f in range(4))
SLABS = sum(WIDTHS)


def gelu_slope(value):
    normal_cdf = 0.5 * (1.0 + lax.erf(value * inv_root_two))
    density = jnp.exp(-0.5 * value * value) * inv_root_two_pi
    return normal_cdf + value * density


def roll(value, shift):
    shift %= LANES
    return pltpu.roll(value, shift, 1) if shift else value


def lane_index(rows):
    return lax.broadcasted_iota(jnp.int32, (rows, LANES), 1)


def vmem(count):
    return [pl.BlockSpec(memory_space=pltpu.VMEM)] * count


def slab_at(ref, depth, rows, row):
    channels = ref.shape[0] // (depth * rows)
    parts = [ref[pl.ds(z * rows + row, channels, stride=depth * rows), :] for z in range(depth)]
    return jnp.concatenate(parts, axis=0)


def split(value):
    high = value.astype(BF16)
    low = (value - high.astype(F32)).astype(BF16)
    return high, low


def pack_kernel(depth, rows, *refs):
    fields, (inner, outer, strip) = refs[:4], refs[4:]
    odd = lax.rem(lax.axis_index("gx"), 2)
    planes = fields[0].shape[0] // rows
    lane = lane_index(planes)
    total = jnp.zeros((planes, LANES), F32)
    for f, ref in enumerate(fields):
        width = WIDTHS[f]
        for j in range(width):
            at = pl.ds((STARTS[f] + j) * planes, planes)
            inner[at, :] = slab_at(ref, depth, rows, (rows - width) * (1 - odd) + j)
            outer[at, :] = slab_at(ref, depth, rows, (rows - width) * odd + j)
        for r in range(rows):
            value = slab_at(ref, depth, rows, r)
            base = (f * rows + r) * SIDE
            first = (lane >= base) & (lane < base + HALO)
            last = (lane >= base + HALO) & (lane < base + SIDE)
            total = jnp.where(first, roll(value, base), total)
            total = jnp.where(last, roll(value, base + SIDE), total)
    strip[...] = total


def weight_kernel(channels, depth, *refs):
    kernels, (forward, backward) = refs[:LAYERS], refs[LAYERS:]
    planes = channels * depth
    in_low = lax.rem(lane_index(channels), planes) < channels
    for layer in range(LAYERS):
        for b in range(3):
            for c in range(3):
                tiles = []
                for a in range(3):
                    tap = kernels[layer][9 * a + 3 * b + c]
                    tiles.append(jnp.concatenate([tap] * (LANES // channels), axis=1))
                upper = jnp.where(in_low, tiles[1], tiles[2])
                lower = jnp.where(in_low, tiles[0], tiles[1])
                whole = jnp.concatenate([upper, lower], axis=0)
                turned = jnp.concatenate([whole, whole], axis=0).T[:planes]
                for ref, value, bb, cc in ((forward, whole, b, c), (backward, turned, 2 - b, 2 - c)):
                    base = (layer * 3 + bb) * 2 * planes
                    high, low = split(value)
                    ref[pl.ds(base, planes), pl.ds(cc * LANES, LANES)] = high
                    ref[pl.ds(base + planes, planes), pl.ds(cc * LANES, LANES)] = low


def main_kernel(depth, rows, channels, gy_rounds, factor, *refs):
    fields = refs[:4]
    inner, outer = refs[4:6]
    strips = refs[6 : 6 + 3 * gy_rounds]
    rest = refs[6 + 3 * gy_rounds :]
    forward, backward, grad_out, keep, send, xs, xside, hs, hside, gsum = rest
    planes = depth * channels
    gx, gy = lax.axis_index("gx"), lax.axis_index("gy")
    gx_size, gy_size = lax.axis_size("gx"), lax.axis_size("gy")
    x_odd, y_odd = lax.rem(gx, 2) == 1, lax.rem(gy, 2) == 1
    lane = lane_index(planes)
    place = lax.rem(lane, SIDE)
    right = place < HALO
    zero = jnp.zeros((planes, LANES), F32)

    def side_strip(group):
        got = [strips[group * gy_rounds + r][...] for r in range(gy_rounds)]
        if gy_rounds == 0:
            return zero
        if gy_rounds == 1:
            got.append(zero)
        from_right = jnp.where(y_odd, got[1], got[0])
        from_left = jnp.where(y_odd, got[0], got[1])
        return jnp.where(right, from_right, from_left)

    own_strip, inner_strip, outer_strip = (side_strip(g) for g in range(3))
    before_strip = jnp.where(x_odd, inner_strip, outer_strip)
    after_strip = jnp.where(x_odd, outer_strip, inner_strip)
    span = rows * SIDE

    def field_parts(f):
        width = WIDTHS[f]
        main = {}
        for j in range(width):
            at = pl.ds((STARTS[f] + j) * planes, planes)
            a, b = inner[at, :], outer[at, :]
            main[HALO - width + j] = jnp.where(x_odd, a, b)
            main[HALO + rows + j] = jnp.where(x_odd, b, a)
        for r in range(rows):
            main[HALO + r] = slab_at(fields[f], depth, rows, r)
        lead = HALO * SIDE
        before = roll(before_strip, lead - span - f * span)
        own = roll(own_strip, lead - f * span)
        after = roll(after_strip, lead + span - f * span)
        side = jnp.where(lane < lead, before, jnp.where(lane < lead + span, own, after))
        side = jnp.where(lane < lead + 2 * span, side, 0.0)
        side = jnp.where(lane >= lead - span, side, 0.0)
        return main, side

    def store_shifted(main, side, into, into_side):
        side_up, side_down = roll(side, -1), roll(side, 1)
        for e, value in main.items():
            base = e * SIDE
            down = jnp.where(lane == 0, roll(side, -(base + SIDE - 1)), roll(value, 1))
            up = jnp.where(lane == LANES - 1, roll(side, LANES - 1 - base), roll(value, -1))
            side_up = jnp.where(lane == base + SIDE - 1, roll(value, base + SIDE - 1), side_up)
            side_down = jnp.where(lane == base, roll(value, base + 1), side_down)
            for c, shifted in enumerate((down, value, up)):
                high, low = split(shifted)
                into[pl.ds(c * LANES, planes), pl.ds(e * LANES, LANES)] = high
                into[pl.ds(c * LANES + planes, planes), pl.ds(e * LANES, LANES)] = low
        for c, shifted in enumerate((side_down, side, side_up)):
            for b in range(3):
                high, low = split(roll(shifted, -(b - 1) * SIDE))
                base = (b * 3 + c) * LANES
                into_side[pl.ds(base, planes), :] = high
                into_side[pl.ds(base + planes, planes), :] = low

    def conv(weights, layer, source, lane_start, count):
        total = None
        for b in range(3):
            kernel = weights[pl.ds((layer * 3 + b) * 2 * planes, 2 * planes), :]
            window = source[:, pl.ds(lane_start + (b - 1) * LANES, count * LANES)]
            term = lax.dot_general(kernel, window, NN, preferred_element_type=F32)
            total = term if total is None else total + term
        return total[:planes] + total[planes:]

    def conv_side(weights, layer, source):
        total = None
        for b in range(3):
            kernel = weights[pl.ds((layer * 3 + b) * 2 * planes, 2 * planes), :]
            window = source[pl.ds(b * 3 * LANES, 3 * LANES), :]
            term = lax.dot_general(kernel, window, NN, preferred_element_type=F32)
            total = term if total is None else total + term
        return total[:planes] + total[planes:]

    def conv_rows(weights, layer, source, low, high):
        out = {}
        for e in range(low, high, 2):
            count = min(2, high - e)
            value = conv(weights, layer, source, e * LANES, count)
            for k in range(count):
                out[e + k] = value[:, k * LANES : (k + 1) * LANES]
        return out

    side_row = lane // SIDE
    row_low = jnp.where(gx > 0, 0, HALO)
    row_high = jnp.where(gx < gx_size - 1, 2 * HALO + rows, HALO + rows)
    col_ok = jnp.where(right, (gy < gy_size - 1).astype(jnp.int32), (gy > 0).astype(jnp.int32))
    side_ok = (side_row >= row_low) & (side_row < row_high) & (col_ok > 0)

    grad_main, grad_side = field_parts(1)
    half = lane_index(channels)
    for layer in range(LAYERS):
        x_main, x_side = field_parts((0, 2, 3)[layer])
        store_shifted(x_main, x_side, xs, xside)
        h_width = LAYERS - layer
        low, high = HALO - h_width, HALO + rows + h_width
        pre = conv_rows(forward, layer, xs, low, high)
        h_main = {}
        for e in range(low, high):
            value = grad_main[e] * gelu_slope(pre[e])
            if e < HALO:
                value = jnp.where(gx > 0, value, 0.0)
            if e >= HALO + rows:
                value = jnp.where(gx < gx_size - 1, value, 0.0)
            h_main[e] = value
        h_side = jnp.where(side_ok, grad_side * gelu_slope(conv_side(forward, layer, xside)), 0.0)
        store_shifted(h_main, h_side, hs, hside)

        own = hs[pl.ds(LANES, 2 * planes), pl.ds(HALO * LANES, rows * LANES)]
        tiles, extra = [], []
        for b in range(3):
            window = xs[:, pl.ds((HALO + b - 1) * LANES, rows * LANES)]
            product = lax.dot_general(own, window, NT, preferred_element_type=F32)
            product = product[:planes] + product[planes:]
            for c in range(3):
                tile = product[:, c * LANES : (c + 1) * LANES]
                tile = (tile + roll(tile, planes)) * factor
                upper, lower = tile[:channels], tile[channels:]
                middle = upper + roll(lower, -channels)
                tiles.append(jnp.where(half < channels, lower, jnp.where(half < 2 * channels, upper, middle)))
        for m in range(7):
            tile = tiles[m]
            if m < 6:
                source, part = tiles[7 + m // 3], m % 3
                tile = jnp.where(half < 3 * channels, tile, roll(source, (3 - part) * channels))
            gsum[pl.ds((layer * 7 + m) * channels, channels), :] = tile

        g_width = h_width - 1
        grad_main = conv_rows(backward, layer, hs, HALO - g_width, HALO + rows + g_width)
        if g_width:
            grad_side = conv_side(backward, layer, hside)

    for r in range(rows):
        for z in range(depth):
            at = pl.ds(z * rows + r, channels, stride=depth * rows)
            grad_out[at, :] = grad_main[HALO + r][z * channels : (z + 1) * channels]
    size = keep.shape[0]
    mine = pl.multiple_of(lax.rem(gx, 2) * size, 8)
    other = pl.multiple_of((1 - lax.rem(gx, 2)) * size, 8)
    keep[...] = gsum[pl.ds(mine, size), :]
    send[...] = gsum[pl.ds(other, size), :]


def unpack_kernel(channels, mine, other, *refs):
    outs, whole = refs[:LAYERS], refs[LAYERS]
    size = mine.shape[0]
    odd = lax.rem(lax.axis_index("gx"), 2)
    whole[pl.ds(pl.multiple_of(odd * size, 8), size), :] = mine[...]
    whole[pl.ds(pl.multiple_of((1 - odd) * size, 8), size), :] = other[...]
    order = (0, 2, 1)
    for layer in range(LAYERS):
        for m in range(7):
            tile = whole[pl.ds((layer * 7 + m) * channels, channels), :]
            for s in range(4):
                if s < 3:
                    tap = 9 * order[s] + m
                elif m < 6:
                    tap = 9 * order[m % 3] + 7 + m // 3
                else:
                    continue
                outs[layer][tap] = roll(tile, -s * channels)[:, :channels]


def pair_rounds(size):
    rounds = []
    for start in range(2):
        pairs = [(i, i + 1) for i in range(start, size - 1, 2)]
        if pairs:
            rounds.append(pairs + [(j, i) for i, j in pairs])
    return rounds


def reduce_halves(keep, send, gx_size, gy_size):
    axes = ("gx", "gy")
    total = gx_size * gy_size
    gx, gy = lax.axis_index("gx"), lax.axis_index("gy")

    def swap(value, bit):
        return lax.ppermute(value, axes, [(i, i ^ bit) for i in range(total)])

    value = keep + swap(send, gy_size)
    size = value.shape[0] // 2
    split_at = gy_size > 1
    bits = [1 << k for k in range(1, gy_size.bit_length() - 1)]
    bits += [gy_size << k for k in range(1, gx_size.bit_length() - 1)]
    if split_at:
        side = gy & 1
        mine = lax.dynamic_slice_in_dim(value, side * size, size, axis=0)
        other = lax.dynamic_slice_in_dim(value, (1 - side) * size, size, axis=0)
        value = mine + swap(other, 1)
    for bit in bits:
        value = value + swap(value, bit)
    if split_at:
        got = swap(value, 1)
        value = jnp.where(side == 0, jnp.concatenate([value, got]), jnp.concatenate([got, value]))
    return value, swap(value, gy_size)


def per_device(input_one, input_two, input_three, cotangent, kernel_one, kernel_two, kernel_three):
    channels, depth, rows, cols = input_one.shape
    gx_size, gy_size = lax.axis_size("gx"), lax.axis_size("gy")
    planes = channels * depth
    factor = 1.0 / math.sqrt(depth * rows * cols * gx_size * gy_size)
    fields = [v.reshape(planes * rows, cols) for v in (input_three, cotangent, input_two, input_one)]
    shape = jax.ShapeDtypeStruct

    inner, outer, strip = pl.pallas_call(
        functools.partial(pack_kernel, depth, rows),
        out_shape=[
            shape((SLABS * planes, cols), F32),
            shape((SLABS * planes, cols), F32),
            shape((planes, cols), F32),
        ],
        in_specs=vmem(4),
        out_specs=vmem(3),
        name="pack",
    )(*fields)

    x_rounds, y_rounds = pair_rounds(gx_size), pair_rounds(gy_size)
    both = ("gx", "gy")

    def diagonal(x_pairs, y_pairs):
        return [(i * gy_size + k, j * gy_size + m) for i, j in x_pairs for k, m in y_pairs]

    outer = lax.ppermute(outer, "gx", x_rounds[1])
    strips_own = [lax.ppermute(strip, "gy", pairs) for pairs in y_rounds]
    strips_outer = [lax.ppermute(strip, both, diagonal(x_rounds[1], pairs)) for pairs in y_rounds]
    inner = lax.ppermute(inner, "gx", x_rounds[0])
    strips_inner = [lax.ppermute(strip, both, diagonal(x_rounds[0], pairs)) for pairs in y_rounds]
    strips = strips_own + strips_inner + strips_outer

    weight_shape = shape((LAYERS * 3 * 2 * planes, 3 * LANES), BF16)
    forward, backward = pl.pallas_call(
        functools.partial(weight_kernel, channels, depth),
        out_shape=[weight_shape, weight_shape],
        in_specs=vmem(LAYERS),
        out_specs=vmem(2),
        cost_estimate=pl.CostEstimate(flops=20_000_000, bytes_accessed=4_000_000, transcendentals=0),
        name="weights",
    )(kernel_three, kernel_two, kernel_one)

    total_rows = LAYERS * 7 * channels
    span = (2 * HALO + rows) * LANES
    grad, keep, send = pl.pallas_call(
        functools.partial(main_kernel, depth, rows, channels, len(y_rounds), factor),
        out_shape=[
            shape((planes * rows, cols), F32),
            shape((total_rows // 2, LANES), F32),
            shape((total_rows // 2, LANES), F32),
        ],
        in_specs=vmem(8 + len(strips)),
        out_specs=vmem(3),
        scratch_shapes=[
            pltpu.VMEM((3 * LANES, span), BF16),
            pltpu.VMEM((9 * LANES, LANES), BF16),
            pltpu.VMEM((3 * LANES, span), BF16),
            pltpu.VMEM((9 * LANES, LANES), BF16),
            pltpu.VMEM((total_rows, LANES), F32),
        ],
        compiler_params=pltpu.CompilerParams(vmem_limit_bytes=40 * 1024 * 1024),
        name="layers",
    )(*fields, inner, outer, *strips, forward, backward)

    mine, other = reduce_halves(keep, send, gx_size, gy_size)
    results = pl.pallas_call(
        functools.partial(unpack_kernel, channels),
        out_shape=[shape(kernel_one.shape, F32)] * LAYERS,
        in_specs=vmem(2),
        out_specs=vmem(LAYERS),
        scratch_shapes=[pltpu.VMEM((total_rows, LANES), F32)],
        name="unpack",
    )(mine, other)
    return (grad.reshape(input_one.shape), results[2], results[1], results[0])


def solution(mesh):
    placed = (
        P(None, None, "gx", "gy"),
        P(None, None, "gx", "gy"),
        P(None, None, "gx", "gy"),
        P(None, None, "gx", "gy"),
        P(),
        P(),
        P(),
    )
    return jax.shard_map(
        per_device,
        mesh=mesh,
        in_specs=placed,
        out_specs=(P(None, None, "gx", "gy"), P(), P(), P()),
        check_vma=False,
    )
```

```python
import functools
import math

import jax
import jax.numpy as jnp
from jax import lax
from jax.experimental import pallas as pl
from jax.experimental.pallas import tpu as pltpu
from jax.sharding import PartitionSpec as P

inv_root_two = 0.7071067811865476
inv_root_two_pi = 0.3989422804014327

LAYERS = 3
HALO = LAYERS + 1
SIDE = 2 * HALO
LANES = 128
F32 = jnp.float32
BF16 = jnp.bfloat16
NN = (((1,), (0,)), ((), ()))
NT = (((1,), (1,)), ((), ()))

WIDTHS = (HALO, HALO - 1, HALO - 1, HALO - 2)
STARTS = tuple(sum(WIDTHS[:f]) for f in range(4))
SLABS = sum(WIDTHS)


def gelu_slope(value):
    normal_cdf = 0.5 * (1.0 + lax.erf(value * inv_root_two))
    density = jnp.exp(-0.5 * value * value) * inv_root_two_pi
    return normal_cdf + value * density


def roll(value, shift):
    shift %= LANES
    return pltpu.roll(value, shift, 1) if shift else value


def lane_index(rows):
    return lax.broadcasted_iota(jnp.int32, (rows, LANES), 1)


def near(value):
    return pltpu.with_memory_space_constraint(value, pltpu.VMEM)


def far(value):
    return pltpu.with_memory_space_constraint(value, pltpu.HBM)


def room(mib):
    return pltpu.CompilerParams(vmem_limit_bytes=mib * 1024 * 1024)


def vmem(count):
    return [pl.BlockSpec(memory_space=pltpu.VMEM)] * count


def slab_at(ref, depth, rows, row):
    channels = ref.shape[0] // (depth * rows)
    parts = [ref[pl.ds(z * rows + row, channels, stride=depth * rows), :] for z in range(depth)]
    return jnp.concatenate(parts, axis=0)


def split(value):
    high = value.astype(BF16)
    low = (value - high.astype(F32)).astype(BF16)
    return high, low


def pack_kernel(depth, rows, *refs):
    count = 4 + LAYERS
    inner, outer, strip = refs[2 * count : 2 * count + 3]
    copies = [
        pltpu.make_async_copy(refs[i], refs[count + i], refs[2 * count + 3].at[i]) for i in range(count)
    ]
    for copy in copies:
        copy.start()
    for copy in copies[:4]:
        copy.wait()
    fields = refs[count : count + 4]
    odd = lax.rem(lax.axis_index("gx"), 2)
    planes = fields[0].shape[0] // rows
    lane = lane_index(planes)
    total = jnp.zeros((planes, LANES), F32)
    for f, ref in enumerate(fields):
        width = WIDTHS[f]
        for j in range(width):
            at = pl.ds((STARTS[f] + j) * planes, planes)
            inner[at, :] = slab_at(ref, depth, rows, (rows - width) * (1 - odd) + j)
            outer[at, :] = slab_at(ref, depth, rows, (rows - width) * odd + j)
        for r in range(rows):
            value = slab_at(ref, depth, rows, r)
            base = (f * rows + r) * SIDE
            first = (lane >= base) & (lane < base + HALO)
            last = (lane >= base + HALO) & (lane < base + SIDE)
            total = jnp.where(first, roll(value, base), total)
            total = jnp.where(last, roll(value, base + SIDE), total)
    strip[...] = total
    for copy in copies[4:]:
        copy.wait()


def weight_kernel(channels, depth, *refs):
    kernels, (forward, backward) = refs[:LAYERS], refs[LAYERS:]
    planes = channels * depth
    in_low = lax.rem(lane_index(channels), planes) < channels
    for layer in range(LAYERS):
        for b in range(3):
            for c in range(3):
                tiles = []
                for a in range(3):
                    tap = kernels[layer][9 * a + 3 * b + c]
                    tiles.append(jnp.concatenate([tap] * (LANES // channels), axis=1))
                upper = jnp.where(in_low, tiles[1], tiles[2])
                lower = jnp.where(in_low, tiles[0], tiles[1])
                whole = jnp.concatenate([upper, lower], axis=0)
                turned = jnp.concatenate([whole, whole], axis=0).T[:planes]
                for ref, value, bb, cc in ((forward, whole, b, c), (backward, turned, 2 - b, 2 - c)):
                    base = (layer * 3 + bb) * 2 * planes
                    high, low = split(value)
                    ref[pl.ds(base, planes), pl.ds(cc * LANES, LANES)] = high
                    ref[pl.ds(base + planes, planes), pl.ds(cc * LANES, LANES)] = low


def conv(weights, layer, source, lane_start, count):
    planes = weights.shape[0] // (LAYERS * 3 * 2)
    total = None
    for b in range(3):
        kernel = weights[pl.ds((layer * 3 + b) * 2 * planes, 2 * planes), :]
        window = source[:, pl.ds(lane_start + (b - 1) * LANES, count * LANES)]
        term = lax.dot_general(kernel, window, NN, preferred_element_type=F32)
        total = term if total is None else total + term
    return total[:planes] + total[planes:]


def conv_rows(weights, layer, source, low, high):
    out = {}
    for e in range(low, high, 2):
        count = min(2, high - e)
        value = conv(weights, layer, source, e * LANES, count)
        for k in range(count):
            out[e + k] = value[:, k * LANES : (k + 1) * LANES]
    return out


def main_kernel(depth, rows, channels, gy_rounds, factor, *refs):
    fields = refs[:4]
    inner, outer = refs[4:6]
    strips = refs[6 : 6 + 3 * gy_rounds]
    rest = refs[6 + 3 * gy_rounds :]
    forward, backward, hs, keep, send, xs, xside, hside, gsum = rest
    planes = depth * channels
    gx, gy = lax.axis_index("gx"), lax.axis_index("gy")
    gx_size, gy_size = lax.axis_size("gx"), lax.axis_size("gy")
    x_odd, y_odd = lax.rem(gx, 2) == 1, lax.rem(gy, 2) == 1
    lane = lane_index(planes)
    place = lax.rem(lane, SIDE)
    right = place < HALO
    zero = jnp.zeros((planes, LANES), F32)

    def side_strip(group):
        got = [strips[group * gy_rounds + r][...] for r in range(gy_rounds)]
        if gy_rounds == 0:
            return zero
        if gy_rounds == 1:
            got.append(zero)
        from_right = jnp.where(y_odd, got[1], got[0])
        from_left = jnp.where(y_odd, got[0], got[1])
        return jnp.where(right, from_right, from_left)

    own_strip, inner_strip, outer_strip = (side_strip(g) for g in range(3))
    before_strip = jnp.where(x_odd, inner_strip, outer_strip)
    after_strip = jnp.where(x_odd, outer_strip, inner_strip)
    span = rows * SIDE

    def field_parts(f):
        width = WIDTHS[f]
        main = {}
        for j in range(width):
            at = pl.ds((STARTS[f] + j) * planes, planes)
            a, b = inner[at, :], outer[at, :]
            main[HALO - width + j] = jnp.where(x_odd, a, b)
            main[HALO + rows + j] = jnp.where(x_odd, b, a)
        for r in range(rows):
            main[HALO + r] = slab_at(fields[f], depth, rows, r)
        lead = HALO * SIDE
        before = roll(before_strip, lead - span - f * span)
        own = roll(own_strip, lead - f * span)
        after = roll(after_strip, lead + span - f * span)
        side = jnp.where(lane < lead, before, jnp.where(lane < lead + span, own, after))
        side = jnp.where(lane < lead + 2 * span, side, 0.0)
        side = jnp.where(lane >= lead - span, side, 0.0)
        return main, side

    def store_shifted(main, side, into, into_side):
        side_up, side_down = roll(side, -1), roll(side, 1)
        for e, value in main.items():
            base = e * SIDE
            down = jnp.where(lane == 0, roll(side, -(base + SIDE - 1)), roll(value, 1))
            up = jnp.where(lane == LANES - 1, roll(side, LANES - 1 - base), roll(value, -1))
            side_up = jnp.where(lane == base + SIDE - 1, roll(value, base + SIDE - 1), side_up)
            side_down = jnp.where(lane == base, roll(value, base + 1), side_down)
            for c, shifted in enumerate((down, value, up)):
                high, low = split(shifted)
                into[pl.ds(c * LANES, planes), pl.ds(e * LANES, LANES)] = high
                into[pl.ds(c * LANES + planes, planes), pl.ds(e * LANES, LANES)] = low
        for c, shifted in enumerate((side_down, side, side_up)):
            for b in range(3):
                high, low = split(roll(shifted, -(b - 1) * SIDE))
                base = (b * 3 + c) * LANES
                into_side[pl.ds(base, planes), :] = high
                into_side[pl.ds(base + planes, planes), :] = low

    def conv_side(weights, layer, source):
        total = None
        for b in range(3):
            kernel = weights[pl.ds((layer * 3 + b) * 2 * planes, 2 * planes), :]
            window = source[pl.ds(b * 3 * LANES, 3 * LANES), :]
            term = lax.dot_general(kernel, window, NN, preferred_element_type=F32)
            total = term if total is None else total + term
        return total[:planes] + total[planes:]

    side_row = lane // SIDE
    row_low = jnp.where(gx > 0, 0, HALO)
    row_high = jnp.where(gx < gx_size - 1, 2 * HALO + rows, HALO + rows)
    col_ok = jnp.where(right, (gy < gy_size - 1).astype(jnp.int32), (gy > 0).astype(jnp.int32))
    side_ok = (side_row >= row_low) & (side_row < row_high) & (col_ok > 0)

    padding = gsum.shape[0] - LAYERS * 7 * channels
    if padding:
        gsum[pl.ds(LAYERS * 7 * channels, padding), :] = jnp.zeros((padding, LANES), F32)
    grad_main, grad_side = field_parts(1)
    half = lane_index(channels)
    for layer in range(LAYERS):
        x_main, x_side = field_parts((0, 2, 3)[layer])
        store_shifted(x_main, x_side, xs, xside)
        h_width = LAYERS - layer
        low, high = HALO - h_width, HALO + rows + h_width
        pre = conv_rows(forward, layer, xs, low, high)
        h_main = {}
        for e in range(low, high):
            value = grad_main[e] * gelu_slope(pre[e])
            if e < HALO:
                value = jnp.where(gx > 0, value, 0.0)
            if e >= HALO + rows:
                value = jnp.where(gx < gx_size - 1, value, 0.0)
            h_main[e] = value
        h_side = jnp.where(side_ok, grad_side * gelu_slope(conv_side(forward, layer, xside)), 0.0)
        store_shifted(h_main, h_side, hs, hside)

        own = hs[pl.ds(LANES, 2 * planes), pl.ds(HALO * LANES, rows * LANES)]
        tiles, extra = [], []
        for b in range(3):
            window = xs[:, pl.ds((HALO + b - 1) * LANES, rows * LANES)]
            product = lax.dot_general(own, window, NT, preferred_element_type=F32)
            product = product[:planes] + product[planes:]
            for c in range(3):
                tile = product[:, c * LANES : (c + 1) * LANES]
                tile = (tile + roll(tile, planes)) * factor
                upper, lower = tile[:channels], tile[channels:]
                middle = upper + roll(lower, -channels)
                tiles.append(jnp.where(half < channels, lower, jnp.where(half < 2 * channels, upper, middle)))
        for m in range(7):
            tile = tiles[m]
            if m < 6:
                source, part = tiles[7 + m // 3], m % 3
                tile = jnp.where(half < 3 * channels, tile, roll(source, (3 - part) * channels))
            gsum[pl.ds((layer * 7 + m) * channels, channels), :] = tile

        g_width = h_width - 1
        if g_width:
            grad_main = conv_rows(backward, layer, hs, HALO - g_width, HALO + rows + g_width)
            grad_side = conv_side(backward, layer, hside)

    size = keep.shape[0] // 4
    core, quad = quad_place(gx, gy)
    for k in range(4):
        piece = lax.bitwise_xor(quad, k) * size
        at = pl.ds(k * size, size)
        keep[at, :] = gsum[pl.ds(pl.multiple_of(core * 4 * size + piece, 8), size), :]
        send[at, :] = gsum[pl.ds(pl.multiple_of((1 - core) * 4 * size + piece, 8), size), :]


def quad_place(gx, gy):
    return lax.rem(gx, 2), lax.rem(gy, 2) + 2 * lax.rem(gx // 2, 2)


def grad_kernel(depth, rows, channels, hs, backward, grad_out):
    grad_main = conv_rows(backward, LAYERS - 1, hs, HALO, HALO + rows)
    for r in range(rows):
        for z in range(depth):
            at = pl.ds(z * rows + r, channels, stride=depth * rows)
            grad_out[at, :] = grad_main[HALO + r][z * channels : (z + 1) * channels]


def unpack_kernel(channels, mine, other, *refs):
    outs, whole = refs[:LAYERS], refs[LAYERS]
    size = mine.shape[0] // 4
    core, quad = quad_place(lax.axis_index("gx"), lax.axis_index("gy"))
    for k in range(4):
        piece = lax.bitwise_xor(quad, k) * size
        at = pl.ds(k * size, size)
        whole[pl.ds(pl.multiple_of(core * 4 * size + piece, 8), size), :] = mine[at, :]
        whole[pl.ds(pl.multiple_of((1 - core) * 4 * size + piece, 8), size), :] = other[at, :]
    order = (0, 2, 1)
    for layer in range(LAYERS):
        for m in range(7):
            tile = whole[pl.ds((layer * 7 + m) * channels, channels), :]
            for s in range(4):
                if s < 3:
                    tap = 9 * order[s] + m
                elif m < 6:
                    tap = 9 * order[m % 3] + 7 + m // 3
                else:
                    continue
                outs[layer][tap] = roll(tile, -s * channels)[:, :channels]


def pair_rounds(size):
    rounds = []
    for start in range(2):
        pairs = [(i, i + 1) for i in range(start, size - 1, 2)]
        if pairs:
            rounds.append(pairs + [(j, i) for i, j in pairs])
    return rounds


def reduce_halves(keep, send, beside, gx_size, gy_size):
    axes = ("gx", "gy")
    total = gx_size * gy_size

    def swap(value, bits):
        return lax.ppermute(value, axes, [(i, i ^ bits) for i in range(total)])

    core, quad = gy_size, (1, 2 * gy_size, 2 * gy_size + 1)
    value = keep + swap(send, core)
    size = value.shape[0] // 4
    pieces = [value[k * size : (k + 1) * size] for k in range(4)]
    got = [swap(pieces[k + 1], quad[k]) for k in range(3)]
    value = (pieces[0] + got[0]) + (got[1] + got[2])
    value, beside = lax.optimization_barrier((value, beside))
    bits = [gy_size << k for k in range(2, gx_size.bit_length() - 1)]
    bits += [1 << k for k in range(1, gy_size.bit_length() - 1)]
    while bits:
        low, *high = bits[:2]
        if high:
            got = [swap(value, b) for b in (low, high[0], low | high[0])]
            value = (value + got[0]) + (got[1] + got[2])
        else:
            value = value + swap(value, low)
        bits = bits[2:]
    value = jnp.concatenate([value] + [swap(value, b) for b in quad])
    return value, swap(value, core), beside


def per_device(input_one, input_two, input_three, cotangent, kernel_one, kernel_two, kernel_three):
    channels, depth, rows, cols = input_one.shape
    gx_size, gy_size = lax.axis_size("gx"), lax.axis_size("gy")
    planes = channels * depth
    factor = 1.0 / math.sqrt(depth * rows * cols * gx_size * gy_size)
    fields = [v.reshape(planes * rows, cols) for v in (input_three, cotangent, input_two, input_one)]
    shape = jax.ShapeDtypeStruct

    kernels = [kernel_three, kernel_two, kernel_one]
    *local, inner, outer, strip = pl.pallas_call(
        functools.partial(pack_kernel, depth, rows),
        out_shape=[pltpu.VMEM(v.shape, F32) for v in fields + kernels]
        + [
            pltpu.VMEM((SLABS * planes, cols), F32),
            pltpu.VMEM((SLABS * planes, cols), F32),
            pltpu.VMEM((planes, cols), F32),
        ],
        in_specs=[pl.BlockSpec(memory_space=pltpu.HBM)] * (4 + LAYERS),
        out_specs=vmem(7 + LAYERS),
        scratch_shapes=[pltpu.SemaphoreType.DMA((4 + LAYERS,))],
        compiler_params=room(8),
        name="pack",
    )(*(far(v) for v in fields + kernels))
    fields, kernels = local[:4], local[4:]

    x_rounds, y_rounds = pair_rounds(gx_size), pair_rounds(gy_size)
    both = ("gx", "gy")

    def diagonal(x_pairs, y_pairs):
        return [(i * gy_size + k, j * gy_size + m) for i, j in x_pairs for k, m in y_pairs]

    outer = lax.ppermute(outer, "gx", x_rounds[1])
    strips_own = [lax.ppermute(strip, "gy", pairs) for pairs in y_rounds]
    strips_outer = [lax.ppermute(strip, both, diagonal(x_rounds[1], pairs)) for pairs in y_rounds]
    inner = lax.ppermute(inner, "gx", x_rounds[0])
    strips_inner = [lax.ppermute(strip, both, diagonal(x_rounds[0], pairs)) for pairs in y_rounds]
    strips = strips_own + strips_inner + strips_outer

    weight_shape = pltpu.VMEM((LAYERS * 3 * 2 * planes, 3 * LANES), BF16)
    forward, backward = pl.pallas_call(
        functools.partial(weight_kernel, channels, depth),
        out_shape=[weight_shape, weight_shape],
        in_specs=vmem(LAYERS),
        out_specs=vmem(2),
        cost_estimate=pl.CostEstimate(flops=20_000_000, bytes_accessed=4_000_000, transcendentals=0),
        compiler_params=room(12),
        name="weights",
    )(*(near(v) for v in kernels))

    tiles = -(-LAYERS * 7 * channels // 64) * 64
    span = (2 * HALO + rows) * LANES
    hs, keep, send = pl.pallas_call(
        functools.partial(main_kernel, depth, rows, channels, len(y_rounds), factor),
        out_shape=[
            pltpu.VMEM((3 * LANES, span), BF16),
            pltpu.VMEM((tiles // 2, LANES), F32),
            pltpu.VMEM((tiles // 2, LANES), F32),
        ],
        in_specs=vmem(8 + len(strips)),
        out_specs=vmem(3),
        scratch_shapes=[
            pltpu.VMEM((3 * LANES, span), BF16),
            pltpu.VMEM((9 * LANES, LANES), BF16),
            pltpu.VMEM((9 * LANES, LANES), BF16),
            pltpu.VMEM((tiles, LANES), F32),
        ],
        compiler_params=room(24),
        name="layers",
    )(*(near(v) for v in (*fields, inner, outer, *strips, forward, backward)))

    grad = pl.pallas_call(
        functools.partial(grad_kernel, depth, rows, channels),
        out_shape=shape((planes * rows, cols), F32),
        in_specs=vmem(2),
        out_specs=vmem(1)[0],
        cost_estimate=pl.CostEstimate(flops=600_000_000, bytes_accessed=1_000_000, transcendentals=0),
        compiler_params=room(8),
        name="grad_input",
    )(near(hs), near(backward))

    mine, other, grad = reduce_halves(keep, send, grad, gx_size, gy_size)
    results = pl.pallas_call(
        functools.partial(unpack_kernel, channels),
        out_shape=[shape(kernel_one.shape, F32)] * LAYERS,
        in_specs=vmem(2),
        out_specs=vmem(LAYERS),
        scratch_shapes=[pltpu.VMEM((tiles, LANES), F32)],
        compiler_params=room(8),
        name="unpack",
    )(near(mine), near(other))
    return (grad.reshape(input_one.shape), results[2], results[1], results[0])


def solution(mesh):
    placed = (
        P(None, None, "gx", "gy"),
        P(None, None, "gx", "gy"),
        P(None, None, "gx", "gy"),
        P(None, None, "gx", "gy"),
        P(),
        P(),
        P(),
    )
    return jax.shard_map(
        per_device,
        mesh=mesh,
        in_specs=placed,
        out_specs=(P(None, None, "gx", "gy"), P(), P(), P()),
        check_vma=False,
    )
```

```python
import functools
import math

import jax
import jax.numpy as jnp
from jax import lax
from jax.experimental import pallas as pl
from jax.experimental.pallas import tpu as pltpu
from jax.sharding import PartitionSpec as P

inv_root_two = 0.7071067811865476
inv_root_two_pi = 0.3989422804014327

LAYERS = 3
HALO = LAYERS + 1
SIDE = 2 * HALO
LANES = 128
F32 = jnp.float32
BF16 = jnp.bfloat16
NN = (((1,), (0,)), ((), ()))
NT = (((1,), (1,)), ((), ()))

WIDTHS = (HALO, HALO - 1, HALO - 1, HALO - 2)
STARTS = tuple(sum(WIDTHS[:f]) for f in range(4))
SLABS = sum(WIDTHS)


def gelu_slope(value):
    normal_cdf = 0.5 * (1.0 + lax.erf(value * inv_root_two))
    density = jnp.exp(-0.5 * value * value) * inv_root_two_pi
    return normal_cdf + value * density


def roll(value, shift):
    shift %= LANES
    return pltpu.roll(value, shift, 1) if shift else value


def lane_index(rows):
    return lax.broadcasted_iota(jnp.int32, (rows, LANES), 1)


def near(value):
    return pltpu.with_memory_space_constraint(value, pltpu.VMEM)


def far(value):
    return pltpu.with_memory_space_constraint(value, pltpu.HBM)


def room(mib):
    return pltpu.CompilerParams(vmem_limit_bytes=mib * 1024 * 1024)


def vmem(count):
    return [pl.BlockSpec(memory_space=pltpu.VMEM)] * count


def slab_at(ref, field, depth, rows, row):
    size = ref.shape[0] // 4
    channels = size // (depth * rows)
    parts = [
        ref[pl.ds(field * size + z * rows + row, channels, stride=depth * rows), :] for z in range(depth)
    ]
    return jnp.concatenate(parts, axis=0)


def split(value):
    high = value.astype(BF16)
    low = (value - high.astype(F32)).astype(BF16)
    return high, low


def fetch_kernel(*refs):
    count = 4 + LAYERS
    sources, (local, *kernels), semaphores = refs[:count], refs[count : count + 1 + LAYERS], refs[-1]
    size = sources[0].shape[0]
    targets = [local.at[pl.ds(f * size, size), :] for f in range(4)] + kernels
    copies = [
        pltpu.make_async_copy(source, target, semaphores.at[k])
        for k, (source, target) in enumerate(zip(sources, targets))
    ]
    for copy in copies:
        copy.start()
    for copy in copies:
        copy.wait()


def pack_kernel(depth, rows, local, sibling, first, second, strips, strip):
    odd = lax.rem(lax.axis_index("gx"), 2)
    planes = local.shape[0] // (4 * rows)
    lane = lane_index(planes)
    for f, width in enumerate(WIDTHS):
        out, start = (first, 0) if f < 2 else (second, STARTS[2])
        for j in range(width):
            row = (rows - width) * (1 - odd) + j
            out[pl.ds((STARTS[f] - start + j) * planes, planes), :] = slab_at(sibling, f, depth, rows, row)
    for k, ref in enumerate((local, sibling)):
        total = jnp.zeros((planes, LANES), F32)
        for f in range(4):
            for r in range(rows):
                value = slab_at(ref, f, depth, rows, r)
                base = (f * rows + r) * SIDE
                leading = (lane >= base) & (lane < base + HALO)
                trailing = (lane >= base + HALO) & (lane < base + SIDE)
                total = jnp.where(leading, roll(value, base), total)
                total = jnp.where(trailing, roll(value, base + SIDE), total)
        strips[pl.ds(k * planes, planes), :] = total
    strip[...] = total


def weight_kernel(channels, depth, *refs):
    kernels, (forward, backward) = refs[:LAYERS], refs[LAYERS:]
    planes = channels * depth
    in_low = lax.rem(lane_index(channels), planes) < channels
    for layer in range(LAYERS):
        for b in range(3):
            for c in range(3):
                tiles = []
                for a in range(3):
                    tap = kernels[layer][9 * a + 3 * b + c]
                    tiles.append(jnp.concatenate([tap] * (LANES // channels), axis=1))
                upper = jnp.where(in_low, tiles[1], tiles[2])
                lower = jnp.where(in_low, tiles[0], tiles[1])
                whole = jnp.concatenate([upper, lower], axis=0)
                turned = jnp.concatenate([whole, whole], axis=0).T[:planes]
                for ref, value, bb, cc in ((forward, whole, b, c), (backward, turned, 2 - b, 2 - c)):
                    base = (layer * 3 + bb) * 2 * planes
                    high, low = split(value)
                    ref[pl.ds(base, planes), pl.ds(cc * LANES, LANES)] = high
                    ref[pl.ds(base + planes, planes), pl.ds(cc * LANES, LANES)] = low


def conv(weights, layer, source, lane_start, count):
    planes = weights.shape[0] // (LAYERS * 3 * 2)
    total = None
    for b in range(3):
        kernel = weights[pl.ds((layer * 3 + b) * 2 * planes, 2 * planes), :]
        window = source[:, pl.ds(lane_start + (b - 1) * LANES, count * LANES)]
        term = lax.dot_general(kernel, window, NN, preferred_element_type=F32)
        total = term if total is None else total + term
    return total[:planes] + total[planes:]


def conv_rows(weights, layer, source, low, high):
    out = {}
    for e in range(low, high, 2):
        count = min(2, high - e)
        value = conv(weights, layer, source, e * LANES, count)
        for k in range(count):
            out[e + k] = value[:, k * LANES : (k + 1) * LANES]
    return out


def layers_kernel(depth, rows, channels, gy_rounds, factor, layers, *refs):
    refs = list(refs)
    take = lambda count: [refs.pop(0) for _ in range(count)]
    opening = layers[0] == 0
    chosen = (0, 1) if opening else (2, 3)
    local, sibling, outer = take(3)
    strips = take(2 * gy_rounds)
    forward, backward = take(2)
    if opening:
        grad_out, sums, xs, xside, hs, hside = refs
    else:
        grad_in, first_sums, hs, keep, send, xs, xside, hside, gsum = refs
    planes = depth * channels
    gx, gy = lax.axis_index("gx"), lax.axis_index("gy")
    gx_size, gy_size = lax.axis_size("gx"), lax.axis_size("gy")
    x_odd, y_odd = lax.rem(gx, 2) == 1, lax.rem(gy, 2) == 1
    odd = lax.rem(gx, 2)
    ended = (gx == 0) | (gx == gx_size - 1)
    lane = lane_index(planes)
    place = lax.rem(lane, SIDE)
    right = place < HALO
    zero = jnp.zeros((planes, LANES), F32)

    def side_strip(group):
        got = []
        for r in range(gy_rounds):
            if group < 2:
                got.append(strips[r][pl.ds(group * planes, planes), :])
            else:
                got.append(jnp.where(ended, 0.0, strips[gy_rounds + r][...]))
        if gy_rounds == 0:
            return zero
        if gy_rounds == 1:
            got.append(zero)
        from_right = jnp.where(y_odd, got[1], got[0])
        from_left = jnp.where(y_odd, got[0], got[1])
        return jnp.where(right, from_right, from_left)

    own_strip, inner_strip, outer_strip = (side_strip(g) for g in range(3))
    before_strip = jnp.where(x_odd, inner_strip, outer_strip)
    after_strip = jnp.where(x_odd, outer_strip, inner_strip)
    span = rows * SIDE

    def field_parts(f):
        width = WIDTHS[f]
        main = {}
        for j in range(width):
            start = STARTS[f] + j - STARTS[chosen[0]]
            a = slab_at(sibling, f, depth, rows, (rows - width) * odd + j)
            b = jnp.where(ended, 0.0, outer[pl.ds(start * planes, planes), :])
            main[HALO - width + j] = jnp.where(x_odd, a, b)
            main[HALO + rows + j] = jnp.where(x_odd, b, a)
        for r in range(rows):
            main[HALO + r] = slab_at(local, f, depth, rows, r)
        lead = HALO * SIDE
        before = roll(before_strip, lead - span - f * span)
        own = roll(own_strip, lead - f * span)
        after = roll(after_strip, lead + span - f * span)
        side = jnp.where(lane < lead, before, jnp.where(lane < lead + span, own, after))
        side = jnp.where(lane < lead + 2 * span, side, 0.0)
        side = jnp.where(lane >= lead - span, side, 0.0)
        return main, side

    def store_shifted(main, side, into, into_side):
        side_up, side_down = roll(side, -1), roll(side, 1)
        for e, value in main.items():
            base = e * SIDE
            down = jnp.where(lane == 0, roll(side, -(base + SIDE - 1)), roll(value, 1))
            up = jnp.where(lane == LANES - 1, roll(side, LANES - 1 - base), roll(value, -1))
            side_up = jnp.where(lane == base + SIDE - 1, roll(value, base + SIDE - 1), side_up)
            side_down = jnp.where(lane == base, roll(value, base + 1), side_down)
            for c, shifted in enumerate((down, value, up)):
                high, low = split(shifted)
                into[pl.ds(c * LANES, planes), pl.ds(e * LANES, LANES)] = high
                into[pl.ds(c * LANES + planes, planes), pl.ds(e * LANES, LANES)] = low
        for c, shifted in enumerate((side_down, side, side_up)):
            for b in range(3):
                high, low = split(roll(shifted, -(b - 1) * SIDE))
                base = (b * 3 + c) * LANES
                into_side[pl.ds(base, planes), :] = high
                into_side[pl.ds(base + planes, planes), :] = low

    def conv_side(weights, layer, source):
        total = None
        for b in range(3):
            kernel = weights[pl.ds((layer * 3 + b) * 2 * planes, 2 * planes), :]
            window = source[pl.ds(b * 3 * LANES, 3 * LANES), :]
            term = lax.dot_general(kernel, window, NN, preferred_element_type=F32)
            total = term if total is None else total + term
        return total[:planes] + total[planes:]

    side_row = lane // SIDE
    row_low = jnp.where(gx > 0, 0, HALO)
    row_high = jnp.where(gx < gx_size - 1, 2 * HALO + rows, HALO + rows)
    col_ok = jnp.where(right, (gy < gy_size - 1).astype(jnp.int32), (gy > 0).astype(jnp.int32))
    side_ok = (side_row >= row_low) & (side_row < row_high) & (col_ok > 0)

    if opening:
        gsum = sums
        grad_main, grad_side = field_parts(1)
    else:
        low = HALO - LAYERS + layers[0]
        count = rows + 2 * (HALO - low)
        grad_main = {low + k: grad_in[pl.ds(k * planes, planes), :] for k in range(count)}
        grad_side = grad_in[pl.ds(count * planes, planes), :]
        done = layers[0] * 7 * channels
        gsum[pl.ds(0, done), :] = first_sums[...]
        padding = gsum.shape[0] - LAYERS * 7 * channels
        if padding:
            gsum[pl.ds(LAYERS * 7 * channels, padding), :] = jnp.zeros((padding, LANES), F32)
    half = lane_index(channels)
    for layer in layers:
        x_main, x_side = field_parts((0, 2, 3)[layer])
        store_shifted(x_main, x_side, xs, xside)
        h_width = LAYERS - layer
        low, high = HALO - h_width, HALO + rows + h_width
        pre = conv_rows(forward, layer, xs, low, high)
        h_main = {}
        for e in range(low, high):
            value = grad_main[e] * gelu_slope(pre[e])
            if e < HALO:
                value = jnp.where(gx > 0, value, 0.0)
            if e >= HALO + rows:
                value = jnp.where(gx < gx_size - 1, value, 0.0)
            h_main[e] = value
        h_side = jnp.where(side_ok, grad_side * gelu_slope(conv_side(forward, layer, xside)), 0.0)
        store_shifted(h_main, h_side, hs, hside)

        own = hs[pl.ds(LANES, 2 * planes), pl.ds(HALO * LANES, rows * LANES)]
        tiles, extra = [], []
        for b in range(3):
            window = xs[:, pl.ds((HALO + b - 1) * LANES, rows * LANES)]
            product = lax.dot_general(own, window, NT, preferred_element_type=F32)
            product = product[:planes] + product[planes:]
            for c in range(3):
                tile = product[:, c * LANES : (c + 1) * LANES]
                tile = (tile + roll(tile, planes)) * factor
                upper, lower = tile[:channels], tile[channels:]
                middle = upper + roll(lower, -channels)
                tiles.append(jnp.where(half < channels, lower, jnp.where(half < 2 * channels, upper, middle)))
        for m in range(7):
            tile = tiles[m]
            if m < 6:
                source, part = tiles[7 + m // 3], m % 3
                tile = jnp.where(half < 3 * channels, tile, roll(source, (3 - part) * channels))
            gsum[pl.ds((layer * 7 + m) * channels, channels), :] = tile

        g_width = h_width - 1
        if g_width:
            grad_main = conv_rows(backward, layer, hs, HALO - g_width, HALO + rows + g_width)
            grad_side = conv_side(backward, layer, hside)

    if opening:
        for k, e in enumerate(sorted(grad_main)):
            grad_out[pl.ds(k * planes, planes), :] = grad_main[e]
        grad_out[pl.ds(len(grad_main) * planes, planes), :] = grad_side
        return
    size = keep.shape[0] // 4
    core, quad = quad_place(gx, gy)
    for k in range(4):
        piece = lax.bitwise_xor(quad, k) * size
        at = pl.ds(k * size, size)
        keep[at, :] = gsum[pl.ds(pl.multiple_of(core * 4 * size + piece, 8), size), :]
        send[at, :] = gsum[pl.ds(pl.multiple_of((1 - core) * 4 * size + piece, 8), size), :]


def quad_place(gx, gy):
    return lax.rem(gx, 2), lax.rem(gy, 2) + 2 * lax.rem(gx // 2, 2)


def grad_kernel(depth, rows, channels, hs, backward, grad_out):
    grad_main = conv_rows(backward, LAYERS - 1, hs, HALO, HALO + rows)
    for r in range(rows):
        for z in range(depth):
            at = pl.ds(z * rows + r, channels, stride=depth * rows)
            grad_out[at, :] = grad_main[HALO + r][z * channels : (z + 1) * channels]


def unpack_kernel(channels, mine, other, *refs):
    outs, whole = refs[:LAYERS], refs[LAYERS]
    size = mine.shape[0] // 4
    core, quad = quad_place(lax.axis_index("gx"), lax.axis_index("gy"))
    for k in range(4):
        piece = lax.bitwise_xor(quad, k) * size
        at = pl.ds(k * size, size)
        whole[pl.ds(pl.multiple_of(core * 4 * size + piece, 8), size), :] = mine[at, :]
        whole[pl.ds(pl.multiple_of((1 - core) * 4 * size + piece, 8), size), :] = other[at, :]
    order = (0, 2, 1)
    for layer in range(LAYERS):
        for m in range(7):
            tile = whole[pl.ds((layer * 7 + m) * channels, channels), :]
            for s in range(4):
                if s < 3:
                    tap = 9 * order[s] + m
                elif m < 6:
                    tap = 9 * order[m % 3] + 7 + m // 3
                else:
                    continue
                outs[layer][tap] = roll(tile, -s * channels)[:, :channels]


def pair_rounds(size):
    rounds = []
    for start in range(2):
        pairs = [(i, i + 1) for i in range(start, size - 1, 2)]
        if pairs:
            rounds.append(pairs + [(j, i) for i, j in pairs])
    return rounds


def reduce_halves(keep, send, beside, gx_size, gy_size):
    axes = ("gx", "gy")
    total = gx_size * gy_size

    def swap(value, bits):
        return lax.ppermute(value, axes, [(i, i ^ bits) for i in range(total)])

    core, quad = gy_size, (1, 2 * gy_size, 2 * gy_size + 1)
    value = keep + swap(send, core)
    size = value.shape[0] // 4
    pieces = [value[k * size : (k + 1) * size] for k in range(4)]
    got = [swap(pieces[k + 1], quad[k]) for k in range(3)]
    value = (pieces[0] + got[0]) + (got[1] + got[2])
    value, beside = lax.optimization_barrier((value, beside))
    bits = [gy_size << k for k in range(2, gx_size.bit_length() - 1)]
    bits += [1 << k for k in range(1, gy_size.bit_length() - 1)]
    while bits:
        low, *high = bits[:2]
        if high:
            got = [swap(value, b) for b in (low, high[0], low | high[0])]
            value = (value + got[0]) + (got[1] + got[2])
        else:
            value = value + swap(value, low)
        bits = bits[2:]
    value = jnp.concatenate([value] + [swap(value, b) for b in quad])
    return value, swap(value, core), beside


def per_device(input_one, input_two, input_three, cotangent, kernel_one, kernel_two, kernel_three):
    channels, depth, rows, cols = input_one.shape
    gx_size, gy_size = lax.axis_size("gx"), lax.axis_size("gy")
    planes = channels * depth
    factor = 1.0 / math.sqrt(depth * rows * cols * gx_size * gy_size)
    fields = [v.reshape(planes * rows, cols) for v in (input_three, cotangent, input_two, input_one)]
    shape = jax.ShapeDtypeStruct

    kernels = [kernel_three, kernel_two, kernel_one]
    size = planes * rows
    local, *kernels = pl.pallas_call(
        fetch_kernel,
        out_shape=[pltpu.VMEM((4 * size, cols), F32)] + [pltpu.VMEM(v.shape, F32) for v in kernels],
        in_specs=[pl.BlockSpec(memory_space=pltpu.HBM)] * (4 + LAYERS),
        out_specs=vmem(1 + LAYERS),
        scratch_shapes=[pltpu.SemaphoreType.DMA((4 + LAYERS,))],
        compiler_params=room(8),
        name="fetch",
    )(*(far(v) for v in fields + kernels))

    sibling = lax.ppermute(local, "gx", [(i, i ^ 1) for i in range(gx_size)])
    across = [(i, i - 2) if i % 2 else (i, i + 2) for i in range(gx_size)]
    across = [(i, j) if 0 <= j < gx_size else (i, i ^ 1) for i, j in across]
    y_rounds = pair_rounds(gy_size)
    first, second, strips, strip = pl.pallas_call(
        functools.partial(pack_kernel, depth, rows),
        out_shape=[
            pltpu.VMEM((STARTS[2] * planes, cols), F32),
            pltpu.VMEM(((SLABS - STARTS[2]) * planes, cols), F32),
            pltpu.VMEM((2 * planes, cols), F32),
            pltpu.VMEM((planes, cols), F32),
        ],
        in_specs=vmem(2),
        out_specs=vmem(4),
        compiler_params=room(8),
        name="pack",
    )(near(local), near(sibling))

    def diagonal(x_pairs, y_pairs):
        return [(i * gy_size + k, j * gy_size + m) for i, j in x_pairs for k, m in y_pairs]

    first = lax.ppermute(first, "gx", across)
    strips = [lax.ppermute(strips, "gy", pairs) for pairs in y_rounds]
    corners = [lax.ppermute(strip, ("gx", "gy"), diagonal(across, pairs)) for pairs in y_rounds]
    second, *strips = lax.optimization_barrier((second, *strips))
    second = lax.ppermute(second, "gx", across)
    strips += corners

    weight_shape = pltpu.VMEM((LAYERS * 3 * 2 * planes, 3 * LANES), BF16)
    forward, backward = pl.pallas_call(
        functools.partial(weight_kernel, channels, depth),
        out_shape=[weight_shape, weight_shape],
        in_specs=vmem(LAYERS),
        out_specs=vmem(2),
        cost_estimate=pl.CostEstimate(flops=20_000_000, bytes_accessed=4_000_000, transcendentals=0),
        compiler_params=room(12),
        name="weights",
    )(*(near(v) for v in kernels))

    tiles = -(-LAYERS * 7 * channels // 64) * 64
    span = (2 * HALO + rows) * LANES
    scratch = [pltpu.VMEM((3 * LANES, span), BF16), pltpu.VMEM((9 * LANES, LANES), BF16)]
    kernel = functools.partial(layers_kernel, depth, rows, channels, len(y_rounds), factor)
    grad, sums = pl.pallas_call(
        functools.partial(kernel, (0,)),
        out_shape=[
            pltpu.VMEM(((rows + 2 * (LAYERS - 1) + 1) * planes, LANES), F32),
            pltpu.VMEM((7 * channels, LANES), F32),
        ],
        in_specs=vmem(5 + len(strips)),
        out_specs=vmem(2),
        scratch_shapes=scratch * 2,
        compiler_params=room(16),
        cost_estimate=pl.CostEstimate(flops=3_000_000_000, bytes_accessed=3_000_000, transcendentals=0),
        name="layer_three",
    )(*(near(v) for v in (local, sibling, first, *strips, forward, backward)))
    hs, keep, send = pl.pallas_call(
        functools.partial(kernel, (1, 2)),
        out_shape=[
            pltpu.VMEM((3 * LANES, span), BF16),
            pltpu.VMEM((tiles // 2, LANES), F32),
            pltpu.VMEM((tiles // 2, LANES), F32),
        ],
        in_specs=vmem(7 + len(strips)),
        out_specs=vmem(3),
        scratch_shapes=scratch + [pltpu.VMEM((9 * LANES, LANES), BF16), pltpu.VMEM((tiles, LANES), F32)],
        compiler_params=room(16),
        name="layers",
    )(*(near(v) for v in (local, sibling, second, *strips, forward, backward, grad, sums)))

    grad = pl.pallas_call(
        functools.partial(grad_kernel, depth, rows, channels),
        out_shape=shape((planes * rows, cols), F32),
        in_specs=vmem(2),
        out_specs=vmem(1)[0],
        cost_estimate=pl.CostEstimate(flops=600_000_000, bytes_accessed=1_000_000, transcendentals=0),
        compiler_params=room(8),
        name="grad_input",
    )(near(hs), near(backward))

    mine, other, grad = reduce_halves(keep, send, grad, gx_size, gy_size)
    results = pl.pallas_call(
        functools.partial(unpack_kernel, channels),
        out_shape=[shape(kernel_one.shape, F32)] * LAYERS,
        in_specs=vmem(2),
        out_specs=vmem(LAYERS),
        scratch_shapes=[pltpu.VMEM((tiles, LANES), F32)],
        compiler_params=room(8),
        name="unpack",
    )(near(mine), near(other))
    return (grad.reshape(input_one.shape), results[2], results[1], results[0])


def solution(mesh):
    placed = (
        P(None, None, "gx", "gy"),
        P(None, None, "gx", "gy"),
        P(None, None, "gx", "gy"),
        P(None, None, "gx", "gy"),
        P(),
        P(),
        P(),
    )
    return jax.shard_map(
        per_device,
        mesh=mesh,
        in_specs=placed,
        out_specs=(P(None, None, "gx", "gy"), P(), P(), P()),
        check_vma=False,
    )
```

```python
import functools
import math

import jax
import jax.numpy as jnp
from jax import lax
from jax.experimental import pallas as pl
from jax.experimental.pallas import tpu as pltpu
from jax.sharding import PartitionSpec as P

inv_root_two = 0.7071067811865476
inv_root_two_pi = 0.3989422804014327

LAYERS = 3
HALO = LAYERS + 1
SIDE = 2 * HALO
LANES = 128
F32 = jnp.float32
BF16 = jnp.bfloat16
NN = (((1,), (0,)), ((), ()))
NT = (((1,), (1,)), ((), ()))

WIDTHS = (LAYERS, LAYERS - 1, LAYERS - 1, LAYERS - 2)
STARTS = tuple(sum(WIDTHS[:f]) for f in range(4))
SLABS = sum(WIDTHS)


def gelu_slope(value):
    normal_cdf = 0.5 * (1.0 + lax.erf(value * inv_root_two))
    density = jnp.exp(-0.5 * value * value) * inv_root_two_pi
    return normal_cdf + value * density


def roll(value, shift):
    shift %= LANES
    return pltpu.roll(value, shift, 1) if shift else value


def lane_index(rows):
    return lax.broadcasted_iota(jnp.int32, (rows, LANES), 1)


def near(value):
    return pltpu.with_memory_space_constraint(value, pltpu.VMEM)


def far(value):
    return pltpu.with_memory_space_constraint(value, pltpu.HBM)


def room(mib):
    return pltpu.CompilerParams(vmem_limit_bytes=mib * 1024 * 1024)


def vmem(count):
    return [pl.BlockSpec(memory_space=pltpu.VMEM)] * count


def slab_at(ref, field, depth, rows, row):
    size = ref.shape[0] // 4
    channels = size // (depth * rows)
    parts = [
        ref[pl.ds(field * size + z * rows + row, channels, stride=depth * rows), :] for z in range(depth)
    ]
    return jnp.concatenate(parts, axis=0)


def split(value):
    high = value.astype(BF16)
    low = (value - high.astype(F32)).astype(BF16)
    return high, low


def fetch_kernel(*refs):
    count = 4 + LAYERS
    sources, (local, *kernels), semaphores = refs[:count], refs[count : count + 1 + LAYERS], refs[-1]
    size = sources[0].shape[0]
    targets = [local.at[pl.ds(f * size, size), :] for f in range(4)] + kernels
    copies = [
        pltpu.make_async_copy(source, target, semaphores.at[k])
        for k, (source, target) in enumerate(zip(sources, targets))
    ]
    for copy in copies:
        copy.start()
    for copy in copies:
        copy.wait()


def pack_rows(depth, rows, sibling, out):
    odd = lax.rem(lax.axis_index("gx"), 2)
    planes = sibling.shape[0] // (4 * rows)
    for f, width in enumerate(WIDTHS):
        for j in range(width):
            row = (rows - width) * (1 - odd) + j
            out[pl.ds((STARTS[f] + j) * planes, planes), :] = slab_at(sibling, f, depth, rows, row)


def pack_strips(depth, rows, local, sibling, strips, strip):
    planes = local.shape[0] // (4 * rows)
    lane = lane_index(planes)
    for k, ref in enumerate((local, sibling)):
        total = jnp.zeros((planes, LANES), F32)
        for f in range(4):
            for r in range(rows):
                value = slab_at(ref, f, depth, rows, r)
                base = (f * rows + r) * SIDE
                here = (lane >= base) & (lane < base + SIDE)
                total = jnp.where(here, roll(value, base + HALO), total)
        strips[pl.ds(k * planes, planes), :] = total
    strip[...] = total


def weight_kernel(channels, depth, *refs):
    kernels, (forward, backward) = refs[:LAYERS], refs[LAYERS:]
    planes = channels * depth
    in_low = lax.rem(lane_index(channels), planes) < channels
    for layer in range(LAYERS):
        for b in range(3):
            for c in range(3):
                tiles = []
                for a in range(3):
                    tap = kernels[layer][9 * a + 3 * b + c]
                    tiles.append(jnp.concatenate([tap] * (LANES // channels), axis=1))
                upper = jnp.where(in_low, tiles[1], tiles[2])
                lower = jnp.where(in_low, tiles[0], tiles[1])
                whole = jnp.concatenate([upper, lower], axis=0)
                turned = jnp.concatenate([whole, whole], axis=0).T[:planes]
                for ref, value, bb, cc in ((forward, whole, b, c), (backward, turned, 2 - b, 2 - c)):
                    base, lanes = layer * 2 * planes, pl.ds((bb * 3 + cc) * LANES, LANES)
                    high, low = split(value)
                    ref[pl.ds(base, planes), lanes] = high
                    ref[pl.ds(base + planes, planes), lanes] = low


def conv(weights, layer, window):
    planes = weights.shape[0] // (LAYERS * 2)
    kernel = weights[pl.ds(layer * 2 * planes, 2 * planes), :]
    total = lax.dot_general(kernel, window, NN, preferred_element_type=F32)
    return total[:planes] + total[planes:]


def conv_rows(weights, layer, source, low, high):
    out = {}
    for e in range(low, high, 2):
        count = min(2, high - e)
        window = [source[:, pl.ds((e + b - 1) * LANES, count * LANES)] for b in range(3)]
        value = conv(weights, layer, jnp.concatenate(window, axis=0))
        for k in range(count):
            out[e + k] = value[:, k * LANES : (k + 1) * LANES]
    return out


def store_shifted(main, side, into, into_side=None):
    planes = side.shape[0]
    lane = lane_index(planes)
    ahead, behind = side, side

    def store(target, c, lanes, value):
        high, low = split(value)
        target[pl.ds(c * LANES, planes), lanes] = high
        target[pl.ds(c * LANES + planes, planes), lanes] = low

    for e, value in main.items():
        base = e * SIDE
        ends = roll(side, -base)
        down = roll(jnp.where(lane == LANES - 1, ends, value), 1)
        up = roll(jnp.where(lane == 0, ends, value), -1)
        for c, shifted in enumerate((down, value, up)):
            store(into, c, pl.ds(e * LANES, LANES), shifted)
        if into_side is not None:
            value = roll(value, base)
            ahead = jnp.where(lane == base, value, ahead)
            behind = jnp.where(lane == (base - 1) % LANES, value, behind)
    if into_side is not None:
        for c, shifted in enumerate((roll(behind, 1), side, roll(ahead, -1))):
            store(into_side, c, pl.ds(0, LANES), shifted)


def conv_side(weights, layer, shifted):
    planes = weights.shape[0] // (LAYERS * 2)
    parts = []
    for b in range(3):
        kernel = weights[pl.ds(layer * 2 * planes, 2 * planes), pl.ds(b * 3 * LANES, 3 * LANES)]
        part = lax.dot_general(kernel, shifted[...], NN, preferred_element_type=F32)
        parts.append(roll(part[:planes] + part[planes:], -(b - 1) * SIDE))
    return parts[0] + parts[1] + parts[2]


def layers_kernel(depth, rows, channels, gy_rounds, factor, *refs):
    local, sibling, outer = refs[:3]
    strips = refs[3 : 3 + 2 * gy_rounds]
    forward, backward, h_out, keep, send, xs, xside, hs, hside, gsum = refs[3 + 2 * gy_rounds :]
    planes = depth * channels
    gx, gy = lax.axis_index("gx"), lax.axis_index("gy")
    gx_size, gy_size = lax.axis_size("gx"), lax.axis_size("gy")
    x_odd, y_odd = lax.rem(gx, 2) == 1, lax.rem(gy, 2) == 1
    odd = lax.rem(gx, 2)
    ended = (gx == 0) | (gx == gx_size - 1)
    lane = lane_index(planes)
    right = lax.rem(lane, SIDE) >= HALO
    zero = jnp.zeros((planes, LANES), F32)

    def side_strip(group):
        got = []
        for r in range(gy_rounds):
            if group < 2:
                got.append(strips[r][pl.ds(group * planes, planes), :])
            else:
                got.append(jnp.where(ended, 0.0, strips[gy_rounds + r][...]))
        if gy_rounds == 0:
            return zero
        if gy_rounds == 1:
            got.append(zero)
        from_right = jnp.where(y_odd, got[1], got[0])
        from_left = jnp.where(y_odd, got[0], got[1])
        return jnp.where(right, from_right, from_left)

    own_strip, inner_strip, outer_strip = (side_strip(g) for g in range(3))
    before_strip = jnp.where(x_odd, inner_strip, outer_strip)
    after_strip = jnp.where(x_odd, outer_strip, inner_strip)
    span = rows * SIDE

    def field_parts(f):
        width = WIDTHS[f]
        main = {}
        for j in range(width):
            start = STARTS[f] + j
            a = slab_at(sibling, f, depth, rows, (rows - width) * odd + j)
            b = jnp.where(ended, 0.0, outer[pl.ds(start * planes, planes), :])
            main[HALO - width + j] = jnp.where(x_odd, a, b)
            main[HALO + rows + j] = jnp.where(x_odd, b, a)
        for r in range(rows):
            main[HALO + r] = slab_at(local, f, depth, rows, r)
        lead = HALO * SIDE - HALO
        before = roll(before_strip, lead - span - f * span)
        own = roll(own_strip, lead - f * span)
        after = roll(after_strip, lead + span - f * span)
        side = jnp.where(lane < lead, before, jnp.where(lane < lead + span, own, after))
        side = jnp.where(lane < lead + 2 * span, side, 0.0)
        return main, side

    side_row = (lane + HALO) // SIDE
    right = lax.rem(lane + HALO, SIDE) >= HALO
    row_low = jnp.where(gx > 0, 0, HALO)
    row_high = jnp.where(gx < gx_size - 1, 2 * HALO + rows, HALO + rows)
    col_ok = jnp.where(right, (gy < gy_size - 1).astype(jnp.int32), (gy > 0).astype(jnp.int32))
    side_ok = (side_row >= row_low) & (side_row < row_high) & (col_ok > 0)

    padding = gsum.shape[0] - LAYERS * 7 * channels
    if padding:
        gsum[pl.ds(LAYERS * 7 * channels, padding), :] = jnp.zeros((padding, LANES), F32)
    grad_main, grad_side = field_parts(1)
    half = lane_index(channels)
    for layer in range(LAYERS):
        x_main, x_side = field_parts((0, 2, 3)[layer])
        store_shifted(x_main, x_side, xs, xside)
        h_width = LAYERS - 1 - layer
        low, high = HALO - h_width, HALO + rows + h_width
        pre = conv_rows(forward, layer, xs, low, high)
        h_main = {}
        for e in range(low, high):
            value = grad_main[e] * gelu_slope(pre[e])
            if e < HALO:
                value = jnp.where(gx > 0, value, 0.0)
            if e >= HALO + rows:
                value = jnp.where(gx < gx_size - 1, value, 0.0)
            h_main[e] = value
        h_side = jnp.where(side_ok, grad_side * gelu_slope(conv_side(forward, layer, xside)), 0.0)
        if h_width:
            store_shifted(h_main, h_side, hs, hside)
            own = hs[pl.ds(LANES, 2 * planes), pl.ds(HALO * LANES, rows * LANES)]
        else:
            parts = [split(h_main[HALO + r]) for r in range(rows)]
            own = [jnp.concatenate([part[k] for part in parts], axis=1) for k in range(2)]
            own = jnp.concatenate(own, axis=0)
        tiles, extra = [], []
        for b in range(3):
            window = xs[:, pl.ds((HALO + b - 1) * LANES, rows * LANES)]
            product = lax.dot_general(own, window, NT, preferred_element_type=F32)
            product = product[:planes] + product[planes:]
            for c in range(3):
                tile = product[:, c * LANES : (c + 1) * LANES]
                tile = (tile + roll(tile, planes)) * factor
                upper, lower = tile[:channels], tile[channels:]
                middle = upper + roll(lower, -channels)
                tiles.append(jnp.where(half < channels, lower, jnp.where(half < 2 * channels, upper, middle)))
        for m in range(7):
            tile = tiles[m]
            if m < 6:
                source, part = tiles[7 + m // 3], m % 3
                tile = jnp.where(half < 3 * channels, tile, roll(source, (3 - part) * channels))
            gsum[pl.ds((layer * 7 + m) * channels, channels), :] = tile

        if h_width:
            g_width = h_width - 1
            grad_main = conv_rows(backward, layer, hs, HALO - g_width, HALO + rows + g_width)
            grad_side = conv_side(backward, layer, hside)

    for r in range(rows):
        h_out[pl.ds(r * planes, planes), :] = h_main[HALO + r]
    h_out[pl.ds(rows * planes, planes), :] = h_side
    head, tail = h_main[HALO], h_main[HALO + rows - 1]
    base = keep.shape[0]
    send[pl.ds(base, planes), :] = jnp.where(x_odd, head, tail)
    send[pl.ds(base + planes, planes), :] = jnp.where(x_odd, tail, head)
    send[pl.ds(base + 2 * planes, planes), :] = h_side
    size = keep.shape[0] // 4
    core, quad = quad_place(gx, gy)
    for k in range(4):
        piece = lax.bitwise_xor(quad, k) * size
        at = pl.ds(k * size, size)
        keep[at, :] = gsum[pl.ds(pl.multiple_of(core * 4 * size + piece, 8), size), :]
        send[at, :] = gsum[pl.ds(pl.multiple_of((1 - core) * 4 * size + piece, 8), size), :]


def quad_place(gx, gy):
    return lax.rem(gx, 2), lax.rem(gy, 2) + 2 * lax.rem(gx // 2, 2)


def grad_kernel(depth, rows, channels, own, swapped, ringed, backward, grad_out, hs):
    planes = depth * channels
    gx, gx_size = lax.axis_index("gx"), lax.axis_size("gx")
    x_odd, ended = lax.rem(gx, 2) == 1, (gx == 0) | (gx == gx_size - 1)
    lane = lane_index(planes)
    span = rows * SIDE
    inner, inner_side = swapped[pl.ds(0, planes), :], swapped[pl.ds(2 * planes, planes), :]
    outer = jnp.where(ended, 0.0, ringed[pl.ds(0, planes), :])
    outer_side = jnp.where(ended, 0.0, ringed[pl.ds(planes, planes), :])
    main = {HALO + r: own[pl.ds(r * planes, planes), :] for r in range(rows)}
    main[HALO - 1] = jnp.where(x_odd, inner, outer)
    main[HALO + rows] = jnp.where(x_odd, outer, inner)
    before = roll(jnp.where(x_odd, inner_side, outer_side), -span)
    after = roll(jnp.where(x_odd, outer_side, inner_side), span)
    side = own[pl.ds(rows * planes, planes), :]
    lead = HALO * SIDE - HALO
    side = jnp.where(lane < lead, before, jnp.where(lane < lead + span, side, after))
    store_shifted(main, side, hs)
    grad_main = conv_rows(backward, LAYERS - 1, hs, HALO, HALO + rows)
    for r in range(rows):
        for z in range(depth):
            at = pl.ds(z * rows + r, channels, stride=depth * rows)
            grad_out[at, :] = grad_main[HALO + r][z * channels : (z + 1) * channels]


def unpack_kernel(channels, mine, other, *refs):
    outs, whole = refs[:LAYERS], refs[LAYERS]
    size = mine.shape[0] // 4
    core, quad = quad_place(lax.axis_index("gx"), lax.axis_index("gy"))
    for k in range(4):
        piece = lax.bitwise_xor(quad, k) * size
        at = pl.ds(k * size, size)
        whole[pl.ds(pl.multiple_of(core * 4 * size + piece, 8), size), :] = mine[at, :]
        whole[pl.ds(pl.multiple_of((1 - core) * 4 * size + piece, 8), size), :] = other[at, :]
    order = (0, 2, 1)
    for layer in range(LAYERS):
        for m in range(7):
            tile = whole[pl.ds((layer * 7 + m) * channels, channels), :]
            for s in range(4):
                if s < 3:
                    tap = 9 * order[s] + m
                elif m < 6:
                    tap = 9 * order[m % 3] + 7 + m // 3
                else:
                    continue
                outs[layer][tap] = roll(tile, -s * channels)[:, :channels]


def pair_rounds(size):
    rounds = []
    for start in range(2):
        pairs = [(i, i + 1) for i in range(start, size - 1, 2)]
        if pairs:
            rounds.append(pairs + [(j, i) for i, j in pairs])
    return rounds


def reduce_halves(keep, send, beside, gx_size, gy_size):
    axes = ("gx", "gy")
    total = gx_size * gy_size

    def swap(value, bits):
        return lax.ppermute(value, axes, [(i, i ^ bits) for i in range(total)])

    core, quad = gy_size, (1, 2 * gy_size, 2 * gy_size + 1)
    got = swap(send, core)
    count = keep.shape[0]
    value, beside = keep + got[:count], beside(got[count:])
    size = value.shape[0] // 4
    pieces = [value[k * size : (k + 1) * size] for k in range(4)]
    got = [swap(pieces[k + 1], quad[k]) for k in range(3)]
    value = (pieces[0] + got[0]) + (got[1] + got[2])
    bits = [gy_size << k for k in range(2, gx_size.bit_length() - 1)]
    bits += [1 << k for k in range(1, gy_size.bit_length() - 1)]
    while bits:
        low, *high = bits[:2]
        if high:
            got = [swap(value, b) for b in (low, high[0], low | high[0])]
            value = (value + got[0]) + (got[1] + got[2])
        else:
            value = value + swap(value, low)
        bits = bits[2:]
    value, beside = lax.optimization_barrier((value, beside))
    value = jnp.concatenate([value] + [swap(value, b) for b in quad])
    return value, swap(value, core), beside


def per_device(input_one, input_two, input_three, cotangent, kernel_one, kernel_two, kernel_three):
    channels, depth, rows, cols = input_one.shape
    gx_size, gy_size = lax.axis_size("gx"), lax.axis_size("gy")
    planes = channels * depth
    factor = 1.0 / math.sqrt(depth * rows * cols * gx_size * gy_size)
    fields = [v.reshape(planes * rows, cols) for v in (input_three, cotangent, input_two, input_one)]
    shape = jax.ShapeDtypeStruct

    kernels = [kernel_three, kernel_two, kernel_one]
    size = planes * rows
    local, *kernels = pl.pallas_call(
        fetch_kernel,
        out_shape=[pltpu.VMEM((4 * size, cols), F32)] + [pltpu.VMEM(v.shape, F32) for v in kernels],
        in_specs=[pl.BlockSpec(memory_space=pltpu.HBM)] * (4 + LAYERS),
        out_specs=vmem(1 + LAYERS),
        scratch_shapes=[pltpu.SemaphoreType.DMA((4 + LAYERS,))],
        compiler_params=room(8),
        name="fetch",
    )(*(far(v) for v in fields + kernels))

    sibling = lax.ppermute(local, "gx", [(i, i ^ 1) for i in range(gx_size)])
    across = [(i, i - 2) if i % 2 else (i, i + 2) for i in range(gx_size)]
    across = [(i, j) if 0 <= j < gx_size else (i, i ^ 1) for i, j in across]
    y_rounds = pair_rounds(gy_size)
    weight_shape = pltpu.VMEM((LAYERS * 2 * planes, 9 * LANES), BF16)
    forward, backward = pl.pallas_call(
        functools.partial(weight_kernel, channels, depth),
        out_shape=[weight_shape, weight_shape],
        in_specs=vmem(LAYERS),
        out_specs=vmem(2),
        cost_estimate=pl.CostEstimate(flops=20_000_000, bytes_accessed=4_000_000, transcendentals=0),
        compiler_params=room(12),
        name="weights",
    )(*(near(v) for v in kernels))

    sibling, forward, backward = lax.optimization_barrier((sibling, forward, backward))
    outer = pl.pallas_call(
        functools.partial(pack_rows, depth, rows),
        out_shape=pltpu.VMEM((SLABS * planes, cols), F32),
        in_specs=vmem(1),
        out_specs=vmem(1)[0],
        compiler_params=room(8),
        name="pack_rows",
    )(near(sibling))
    strips, strip = pl.pallas_call(
        functools.partial(pack_strips, depth, rows),
        out_shape=[pltpu.VMEM((2 * planes, cols), F32), pltpu.VMEM((planes, cols), F32)],
        in_specs=vmem(2),
        out_specs=vmem(2),
        compiler_params=room(8),
        cost_estimate=pl.CostEstimate(flops=5_000_000, bytes_accessed=2_000_000, transcendentals=0),
        name="pack_strips",
    )(near(local), near(sibling))

    def diagonal(x_pairs, y_pairs):
        return [(i * gy_size + k, j * gy_size + m) for i, j in x_pairs for k, m in y_pairs]

    outer = lax.ppermute(outer, "gx", across)
    corners = [lax.ppermute(strip, ("gx", "gy"), diagonal(across, pairs)) for pairs in y_rounds]
    strips = [lax.ppermute(strips, "gy", pairs) for pairs in y_rounds] + corners

    tiles = -(-LAYERS * 7 * channels // 64) * 64
    span = (2 * HALO + rows) * LANES
    shifted, shifted_side = pltpu.VMEM((3 * LANES, span), BF16), pltpu.VMEM((3 * LANES, LANES), BF16)
    h_own, keep, send = pl.pallas_call(
        functools.partial(layers_kernel, depth, rows, channels, len(y_rounds), factor),
        out_shape=[
            pltpu.VMEM(((rows + 1) * planes, LANES), F32),
            pltpu.VMEM((tiles // 2, LANES), F32),
            pltpu.VMEM((tiles // 2 + 3 * planes, LANES), F32),
        ],
        in_specs=vmem(5 + len(strips)),
        out_specs=vmem(3),
        scratch_shapes=[shifted, shifted_side] * 2 + [pltpu.VMEM((tiles, LANES), F32)],
        compiler_params=room(16),
        name="layers",
    )(*(near(v) for v in (local, sibling, outer, *strips, forward, backward)))

    def input_gradient(swapped):
        ringed = lax.ppermute(swapped[planes:], "gx", across)
        return pl.pallas_call(
            functools.partial(grad_kernel, depth, rows, channels),
            out_shape=shape((planes * rows, cols), F32),
            in_specs=vmem(4),
            out_specs=vmem(1)[0],
            scratch_shapes=[shifted],
            compiler_params=room(8),
            cost_estimate=pl.CostEstimate(flops=600_000_000, bytes_accessed=1_000_000, transcendentals=0),
            name="grad_input",
        )(near(h_own), near(swapped), near(ringed), near(backward))

    mine, other, grad = reduce_halves(keep, send, input_gradient, gx_size, gy_size)
    results = pl.pallas_call(
        functools.partial(unpack_kernel, channels),
        out_shape=[shape(kernel_one.shape, F32)] * LAYERS,
        in_specs=vmem(2),
        out_specs=vmem(LAYERS),
        scratch_shapes=[pltpu.VMEM((tiles, LANES), F32)],
        compiler_params=room(8),
        name="unpack",
    )(near(mine), near(other))
    return (grad.reshape(input_one.shape), results[2], results[1], results[0])


def solution(mesh):
    placed = (
        P(None, None, "gx", "gy"),
        P(None, None, "gx", "gy"),
        P(None, None, "gx", "gy"),
        P(None, None, "gx", "gy"),
        P(),
        P(),
        P(),
    )
    return jax.shard_map(
        per_device,
        mesh=mesh,
        in_specs=placed,
        out_specs=(P(None, None, "gx", "gy"), P(), P(), P()),
        check_vma=False,
    )
```

```python
import functools
import math

import jax
import jax.numpy as jnp
from jax import lax
from jax.experimental import pallas as pl
from jax.experimental.pallas import tpu as pltpu
from jax.sharding import PartitionSpec as P

inv_root_two = 0.7071067811865476
inv_root_two_pi = 0.3989422804014327

LAYERS = 3
HALO = LAYERS + 1
SIDE = 2 * HALO
LANES = 128
F32 = jnp.float32
BF16 = jnp.bfloat16
NN = (((1,), (0,)), ((), ()))
NT = (((1,), (1,)), ((), ()))

WIDTHS = (LAYERS, LAYERS - 1, LAYERS - 1, LAYERS - 2)
STARTS = tuple(sum(WIDTHS[:f]) for f in range(4))
SLABS = sum(WIDTHS)


def gelu_slope(value):
    normal_cdf = 0.5 * (1.0 + lax.erf(value * inv_root_two))
    density = jnp.exp(-0.5 * value * value) * inv_root_two_pi
    return normal_cdf + value * density


def roll(value, shift):
    if not isinstance(shift, int):
        return pltpu.roll(value, lax.rem(shift + LANES, LANES), 1)
    shift %= LANES
    return pltpu.roll(value, shift, 1) if shift else value


def lane_index(rows):
    return lax.broadcasted_iota(jnp.int32, (rows, LANES), 1)


def near(value):
    return pltpu.with_memory_space_constraint(value, pltpu.VMEM)


def far(value):
    return pltpu.with_memory_space_constraint(value, pltpu.HBM)


def room(mib):
    return pltpu.CompilerParams(vmem_limit_bytes=mib * 1024 * 1024)


def vmem(count):
    return [pl.BlockSpec(memory_space=pltpu.VMEM)] * count


def slab_at(ref, field, depth, rows, row):
    size = ref.shape[0] // 4
    channels = size // (depth * rows)
    parts = [
        ref[pl.ds(field * size + z * rows + row, channels, stride=depth * rows), :] for z in range(depth)
    ]
    return jnp.concatenate(parts, axis=0)


def split(value):
    high = value.astype(BF16)
    low = (value - high.astype(F32)).astype(BF16)
    return high, low


def fetch_kernel(*refs):
    count = 4 + LAYERS
    sources, (local, *kernels), semaphores = refs[:count], refs[count : count + 1 + LAYERS], refs[-1]
    size = sources[0].shape[0]
    targets = [local.at[pl.ds(f * size, size), :] for f in range(4)] + kernels
    copies = [
        pltpu.make_async_copy(source, target, semaphores.at[k])
        for k, (source, target) in enumerate(zip(sources, targets))
    ]
    for copy in copies:
        copy.start()
    for copy in copies:
        copy.wait()


def pack_rows(depth, rows, sibling, out):
    odd = lax.rem(lax.axis_index("gx"), 2)
    planes = sibling.shape[0] // (4 * rows)
    for f, width in enumerate(WIDTHS):
        for j in range(width):
            row = (rows - width) * (1 - odd) + j
            out[pl.ds((STARTS[f] + j) * planes, planes), :] = slab_at(sibling, f, depth, rows, row)


def pack_strips(depth, rows, local, sibling, strips, strip):
    planes = local.shape[0] // (4 * rows)
    lane = lane_index(planes)
    for k, ref in enumerate((local, sibling)):
        total = jnp.zeros((planes, LANES), F32)
        for f in range(4):
            for r in range(rows):
                value = slab_at(ref, f, depth, rows, r)
                base = (f * rows + r) * SIDE
                here = (lane >= base) & (lane < base + SIDE)
                total = jnp.where(here, roll(value, base + HALO), total)
        strips[pl.ds(k * planes, planes), :] = total
    strip[...] = total


def weight_kernel(channels, depth, *refs):
    kernels, (forward, backward) = refs[:LAYERS], refs[LAYERS:]
    planes = channels * depth
    in_low = lax.rem(lane_index(channels), planes) < channels
    for layer in range(LAYERS):
        for b in range(3):
            for c in range(3):
                tiles = []
                for a in range(3):
                    tap = kernels[layer][9 * a + 3 * b + c]
                    tiles.append(jnp.concatenate([tap] * (LANES // channels), axis=1))
                upper = jnp.where(in_low, tiles[1], tiles[2])
                lower = jnp.where(in_low, tiles[0], tiles[1])
                whole = jnp.concatenate([upper, lower], axis=0)
                turned = jnp.concatenate([whole, whole], axis=0).T[:planes]
                for ref, value, bb, cc in ((forward, whole, b, c), (backward, turned, 2 - b, 2 - c)):
                    base, lanes = layer * 2 * planes, pl.ds((bb * 3 + cc) * LANES, LANES)
                    high, low = split(value)
                    ref[pl.ds(base, planes), lanes] = high
                    ref[pl.ds(base + planes, planes), lanes] = low


def conv(weights, layer, window):
    planes = weights.shape[0] // (LAYERS * 2)
    kernel = weights[pl.ds(layer * 2 * planes, 2 * planes), :]
    total = lax.dot_general(kernel, window, NN, preferred_element_type=F32)
    return total[:planes] + total[planes:]


def conv_rows(weights, layer, source, low, high):
    out = {}
    for e in range(low, high, 2):
        count = min(2, high - e)
        window = [source[:, pl.ds((e + b - 1) * LANES, count * LANES)] for b in range(3)]
        value = conv(weights, layer, jnp.concatenate(window, axis=0))
        for k in range(count):
            out[e + k] = value[:, k * LANES : (k + 1) * LANES]
    return out


def store_split(target, c, lanes, value):
    planes = value.shape[0]
    high, low = split(value)
    target[pl.ds(c * LANES, planes), lanes] = high
    target[pl.ds(c * LANES + planes, planes), lanes] = low


def shift_rows(main, side, into, edges=None):
    lane = lane_index(side.shape[0])
    for e, value in main:
        base, start = e * SIDE, e * LANES
        if not isinstance(e, int):
            start = pl.multiple_of(start, LANES)
        ends = roll(side, -base)
        down = roll(jnp.where(lane == LANES - 1, ends, value), 1)
        up = roll(jnp.where(lane == 0, ends, value), -1)
        for c, shifted in enumerate((down, value, up)):
            store_split(into, c, pl.ds(start, LANES), shifted)
        if edges is not None:
            edges = jnp.where((lane == base) | (lane == base - 1), roll(value, base), edges)
    return edges


def shift_side(side, edges, into):
    place = lax.rem(lane_index(side.shape[0]), SIDE)
    ahead = roll(jnp.where(place == 0, edges, side), -1)
    behind = roll(jnp.where(place == SIDE - 1, edges, side), 1)
    for c, shifted in enumerate((behind, side, ahead)):
        store_split(into, c, pl.ds(0, LANES), shifted)


def side_strips(got, y_odd):
    zero = jnp.zeros_like(got[0])
    got = (got + [zero])[:2]
    from_right = jnp.where(y_odd, got[1], got[0])
    from_left = jnp.where(y_odd, got[0], got[1])
    return jnp.where(lax.rem(lane_index(zero.shape[0]), SIDE) >= HALO, from_right, from_left)


def field_side(f, rows, before, own, after):
    lane = lane_index(own.shape[0])
    span, lead = rows * SIDE, HALO * SIDE - HALO
    before = roll(before, lead - span - f * span)
    after = roll(after, lead + span - f * span)
    side = jnp.where(lane < lead + span, roll(own, lead - f * span), after)
    side = jnp.where(lane < lead, before, side)
    return jnp.where(lane < lead + 2 * span, side, 0.0)


INPUTS = (0, 2, 3)


def early_kernel(depth, rows, *refs):
    local, sibling, *strips = refs[: -2 * LAYERS]
    shifted, edges = refs[-2 * LAYERS : -LAYERS], refs[-LAYERS:]
    planes = local.shape[0] // (4 * rows)
    odd = lax.rem(lax.axis_index("gx"), 2)
    y_odd = lax.rem(lax.axis_index("gy"), 2) == 1
    own, inner = (side_strips([v[pl.ds(k * planes, planes), :] for v in strips], y_odd) for k in range(2))
    for layer, f in enumerate(INPUTS):
        width = WIDTHS[f]
        side = field_side(f, rows, inner, own, inner)
        main = [(HALO + r, slab_at(local, f, depth, rows, r)) for r in range(rows)]
        for j in range(width):
            e = odd * (HALO - width) + (1 - odd) * (HALO + rows) + j
            main.append((e, slab_at(sibling, f, depth, rows, (rows - width) * odd + j)))
        zero = jnp.zeros((planes, LANES), F32)
        edges[layer][...] = shift_rows(main, side, shifted[layer], zero)


def conv_side(weights, layer, shifted):
    planes = weights.shape[0] // (LAYERS * 2)
    parts = []
    for b in range(3):
        kernel = weights[pl.ds(layer * 2 * planes, 2 * planes), pl.ds(b * 3 * LANES, 3 * LANES)]
        part = lax.dot_general(kernel, shifted[...], NN, preferred_element_type=F32)
        parts.append(roll(part[:planes] + part[planes:], -(b - 1) * SIDE))
    return parts[0] + parts[1] + parts[2]


def layers_kernel(depth, rows, channels, gy_rounds, factor, *refs):
    refs = list(refs)
    take = lambda count: [refs.pop(0) for _ in range(count)]
    local, sibling, outer = take(3)
    strips, corners = take(gy_rounds), take(gy_rounds)
    forward, backward = take(2)
    early_edges = take(LAYERS)
    take(LAYERS)
    h_out, keep, send = take(3)
    shifted = take(LAYERS)
    xside, hs, hside, gsum = refs
    planes = depth * channels
    gx, gy = lax.axis_index("gx"), lax.axis_index("gy")
    gx_size, gy_size = lax.axis_size("gx"), lax.axis_size("gy")
    x_odd, y_odd = lax.rem(gx, 2) == 1, lax.rem(gy, 2) == 1
    odd = lax.rem(gx, 2)
    ended = (gx == 0) | (gx == gx_size - 1)
    lane = lane_index(planes)

    own, inner = (side_strips([v[pl.ds(k * planes, planes), :] for v in strips], y_odd) for k in range(2))
    corner = jnp.where(ended, 0.0, side_strips([v[...] for v in corners], y_odd))
    before, after = jnp.where(x_odd, inner, corner), jnp.where(x_odd, corner, inner)

    def outer_row(f, j):
        value = outer[pl.ds((STARTS[f] + j) * planes, planes), :]
        return jnp.where(ended, 0.0, value)

    def cotangent_rows():
        f, main = 1, {}
        width = WIDTHS[f]
        for j in range(width):
            a = slab_at(sibling, f, depth, rows, (rows - width) * odd + j)
            b = outer_row(f, j)
            main[HALO - width + j] = jnp.where(x_odd, a, b)
            main[HALO + rows + j] = jnp.where(x_odd, b, a)
        for r in range(rows):
            main[HALO + r] = slab_at(local, f, depth, rows, r)
        return main

    side_row = (lane + HALO) // SIDE
    right = lax.rem(lane + HALO, SIDE) >= HALO
    row_low = jnp.where(gx > 0, 0, HALO)
    row_high = jnp.where(gx < gx_size - 1, 2 * HALO + rows, HALO + rows)
    col_ok = jnp.where(right, (gy < gy_size - 1).astype(jnp.int32), (gy > 0).astype(jnp.int32))
    side_ok = (side_row >= row_low) & (side_row < row_high) & (col_ok > 0)

    padding = gsum.shape[0] - LAYERS * 7 * channels
    if padding:
        gsum[pl.ds(LAYERS * 7 * channels, padding), :] = jnp.zeros((padding, LANES), F32)
    grad_main, grad_side = cotangent_rows(), field_side(1, rows, before, own, after)
    half = lane_index(channels)
    for layer in range(LAYERS):
        f, xs = INPUTS[layer], shifted[layer]
        x_side = field_side(f, rows, before, own, after)
        x_main = []
        for j in range(WIDTHS[f]):
            e = (1 - odd) * (HALO - WIDTHS[f]) + odd * (HALO + rows) + j
            x_main.append((e, outer_row(f, j)))
        shift_side(x_side, shift_rows(x_main, x_side, xs, early_edges[layer][...]), xside)
        h_width = LAYERS - 1 - layer
        low, high = HALO - h_width, HALO + rows + h_width
        pre = conv_rows(forward, layer, xs, low, high)
        h_main = {}
        for e in range(low, high):
            value = grad_main[e] * gelu_slope(pre[e])
            if e < HALO:
                value = jnp.where(gx > 0, value, 0.0)
            if e >= HALO + rows:
                value = jnp.where(gx < gx_size - 1, value, 0.0)
            h_main[e] = value
        h_side = jnp.where(side_ok, grad_side * gelu_slope(conv_side(forward, layer, xside)), 0.0)
        if h_width:
            edges = shift_rows(h_main.items(), h_side, hs, jnp.zeros((planes, LANES), F32))
            shift_side(h_side, edges, hside)
            center = hs[pl.ds(LANES, 2 * planes), pl.ds(HALO * LANES, rows * LANES)]
        else:
            parts = [split(h_main[HALO + r]) for r in range(rows)]
            center = [jnp.concatenate([part[k] for part in parts], axis=1) for k in range(2)]
            center = jnp.concatenate(center, axis=0)
        tiles, extra = [], []
        for b in range(3):
            window = xs[:, pl.ds((HALO + b - 1) * LANES, rows * LANES)]
            product = lax.dot_general(center, window, NT, preferred_element_type=F32)
            product = product[:planes] + product[planes:]
            for c in range(3):
                tile = product[:, c * LANES : (c + 1) * LANES]
                tile = (tile + roll(tile, planes)) * factor
                upper, lower = tile[:channels], tile[channels:]
                middle = upper + roll(lower, -channels)
                tiles.append(jnp.where(half < channels, lower, jnp.where(half < 2 * channels, upper, middle)))
        for m in range(7):
            tile = tiles[m]
            if m < 6:
                source, part = tiles[7 + m // 3], m % 3
                tile = jnp.where(half < 3 * channels, tile, roll(source, (3 - part) * channels))
            gsum[pl.ds((layer * 7 + m) * channels, channels), :] = tile

        if h_width:
            g_width = h_width - 1
            grad_main = conv_rows(backward, layer, hs, HALO - g_width, HALO + rows + g_width)
            grad_side = conv_side(backward, layer, hside)

    for r in range(rows):
        h_out[pl.ds(r * planes, planes), :] = h_main[HALO + r]
    h_out[pl.ds(rows * planes, planes), :] = h_side
    head, tail = h_main[HALO], h_main[HALO + rows - 1]
    base = keep.shape[0]
    send[pl.ds(base, planes), :] = jnp.where(x_odd, head, tail)
    send[pl.ds(base + planes, planes), :] = jnp.where(x_odd, tail, head)
    send[pl.ds(base + 2 * planes, planes), :] = h_side
    size = keep.shape[0] // 4
    core, quad = quad_place(gx, gy)
    for k in range(4):
        piece = lax.bitwise_xor(quad, k) * size
        at = pl.ds(k * size, size)
        keep[at, :] = gsum[pl.ds(pl.multiple_of(core * 4 * size + piece, 8), size), :]
        send[at, :] = gsum[pl.ds(pl.multiple_of((1 - core) * 4 * size + piece, 8), size), :]


def quad_place(gx, gy):
    return lax.rem(gx, 2), lax.rem(gy, 2) + 2 * lax.rem(gx // 2, 2)


def grad_kernel(depth, rows, channels, own, swapped, ringed, backward, grad_out, hs):
    planes = depth * channels
    gx, gx_size = lax.axis_index("gx"), lax.axis_size("gx")
    x_odd, ended = lax.rem(gx, 2) == 1, (gx == 0) | (gx == gx_size - 1)
    lane = lane_index(planes)
    span = rows * SIDE
    inner, inner_side = swapped[pl.ds(0, planes), :], swapped[pl.ds(2 * planes, planes), :]
    outer = jnp.where(ended, 0.0, ringed[pl.ds(0, planes), :])
    outer_side = jnp.where(ended, 0.0, ringed[pl.ds(planes, planes), :])
    main = {HALO + r: own[pl.ds(r * planes, planes), :] for r in range(rows)}
    main[HALO - 1] = jnp.where(x_odd, inner, outer)
    main[HALO + rows] = jnp.where(x_odd, outer, inner)
    before = roll(jnp.where(x_odd, inner_side, outer_side), -span)
    after = roll(jnp.where(x_odd, outer_side, inner_side), span)
    side = own[pl.ds(rows * planes, planes), :]
    lead = HALO * SIDE - HALO
    side = jnp.where(lane < lead, before, jnp.where(lane < lead + span, side, after))
    shift_rows(main.items(), side, hs)
    grad_main = conv_rows(backward, LAYERS - 1, hs, HALO, HALO + rows)
    for r in range(rows):
        for z in range(depth):
            at = pl.ds(z * rows + r, channels, stride=depth * rows)
            grad_out[at, :] = grad_main[HALO + r][z * channels : (z + 1) * channels]


def unpack_kernel(channels, mine, other, *refs):
    outs, whole = refs[:LAYERS], refs[LAYERS]
    size = mine.shape[0] // 4
    core, quad = quad_place(lax.axis_index("gx"), lax.axis_index("gy"))
    for k in range(4):
        piece = lax.bitwise_xor(quad, k) * size
        at = pl.ds(k * size, size)
        whole[pl.ds(pl.multiple_of(core * 4 * size + piece, 8), size), :] = mine[at, :]
        whole[pl.ds(pl.multiple_of((1 - core) * 4 * size + piece, 8), size), :] = other[at, :]
    order = (0, 2, 1)
    for layer in range(LAYERS):
        for m in range(7):
            tile = whole[pl.ds((layer * 7 + m) * channels, channels), :]
            for s in range(4):
                if s < 3:
                    tap = 9 * order[s] + m
                elif m < 6:
                    tap = 9 * order[m % 3] + 7 + m // 3
                else:
                    continue
                outs[layer][tap] = roll(tile, -s * channels)[:, :channels]


def pair_rounds(size):
    rounds = []
    for start in range(2):
        pairs = [(i, i + 1) for i in range(start, size - 1, 2)]
        if pairs:
            rounds.append(pairs + [(j, i) for i, j in pairs])
    return rounds


def reduce_halves(keep, send, beside, gx_size, gy_size):
    axes = ("gx", "gy")
    total = gx_size * gy_size

    def swap(value, bits):
        return lax.ppermute(value, axes, [(i, i ^ bits) for i in range(total)])

    core, quad = gy_size, (1, 2 * gy_size, 2 * gy_size + 1)
    got = swap(send, core)
    count = keep.shape[0]
    value, beside = keep + got[:count], beside(got[count:])
    size = value.shape[0] // 4
    pieces = [value[k * size : (k + 1) * size] for k in range(4)]
    got = [swap(pieces[k + 1], quad[k]) for k in range(3)]
    value = (pieces[0] + got[0]) + (got[1] + got[2])
    bits = [gy_size << k for k in range(2, gx_size.bit_length() - 1)]
    bits += [1 << k for k in range(1, gy_size.bit_length() - 1)]
    while bits:
        low, *high = bits[:2]
        if high:
            got = [swap(value, b) for b in (low, high[0], low | high[0])]
            value = (value + got[0]) + (got[1] + got[2])
        else:
            value = value + swap(value, low)
        bits = bits[2:]
    value, beside = lax.optimization_barrier((value, beside))
    value = jnp.concatenate([value] + [swap(value, b) for b in quad])
    return value, swap(value, core), beside


def per_device(input_one, input_two, input_three, cotangent, kernel_one, kernel_two, kernel_three):
    channels, depth, rows, cols = input_one.shape
    gx_size, gy_size = lax.axis_size("gx"), lax.axis_size("gy")
    planes = channels * depth
    factor = 1.0 / math.sqrt(depth * rows * cols * gx_size * gy_size)
    fields = [v.reshape(planes * rows, cols) for v in (input_three, cotangent, input_two, input_one)]
    shape = jax.ShapeDtypeStruct

    kernels = [kernel_three, kernel_two, kernel_one]
    size = planes * rows
    local, *kernels = pl.pallas_call(
        fetch_kernel,
        out_shape=[pltpu.VMEM((4 * size, cols), F32)] + [pltpu.VMEM(v.shape, F32) for v in kernels],
        in_specs=[pl.BlockSpec(memory_space=pltpu.HBM)] * (4 + LAYERS),
        out_specs=vmem(1 + LAYERS),
        scratch_shapes=[pltpu.SemaphoreType.DMA((4 + LAYERS,))],
        compiler_params=room(8),
        name="fetch",
    )(*(far(v) for v in fields + kernels))

    sibling = lax.ppermute(local, "gx", [(i, i ^ 1) for i in range(gx_size)])
    across = [(i, i - 2) if i % 2 else (i, i + 2) for i in range(gx_size)]
    across = [(i, j) if 0 <= j < gx_size else (i, i ^ 1) for i, j in across]
    y_rounds = pair_rounds(gy_size)
    weight_shape = pltpu.VMEM((LAYERS * 2 * planes, 9 * LANES), BF16)
    forward, backward = pl.pallas_call(
        functools.partial(weight_kernel, channels, depth),
        out_shape=[weight_shape, weight_shape],
        in_specs=vmem(LAYERS),
        out_specs=vmem(2),
        cost_estimate=pl.CostEstimate(flops=20_000_000, bytes_accessed=4_000_000, transcendentals=0),
        compiler_params=room(12),
        name="weights",
    )(*(near(v) for v in kernels))

    sibling, forward, backward = lax.optimization_barrier((sibling, forward, backward))
    outer = pl.pallas_call(
        functools.partial(pack_rows, depth, rows),
        out_shape=pltpu.VMEM((SLABS * planes, cols), F32),
        in_specs=vmem(1),
        out_specs=vmem(1)[0],
        compiler_params=room(8),
        name="pack_rows",
    )(near(sibling))
    strips, strip = pl.pallas_call(
        functools.partial(pack_strips, depth, rows),
        out_shape=[pltpu.VMEM((2 * planes, cols), F32), pltpu.VMEM((planes, cols), F32)],
        in_specs=vmem(2),
        out_specs=vmem(2),
        compiler_params=room(8),
        cost_estimate=pl.CostEstimate(flops=5_000_000, bytes_accessed=2_000_000, transcendentals=0),
        name="pack_strips",
    )(near(local), near(sibling))

    def diagonal(x_pairs, y_pairs):
        return [(i * gy_size + k, j * gy_size + m) for i, j in x_pairs for k, m in y_pairs]

    outer = lax.ppermute(outer, "gx", across)
    corners = [lax.ppermute(strip, ("gx", "gy"), diagonal(across, pairs)) for pairs in y_rounds]
    strips = [lax.ppermute(strips, "gy", pairs) for pairs in y_rounds]

    tiles = -(-LAYERS * 7 * channels // 64) * 64
    span = (2 * HALO + rows) * LANES
    shifted, shifted_side = pltpu.VMEM((3 * LANES, span), BF16), pltpu.VMEM((3 * LANES, LANES), BF16)
    early = pl.pallas_call(
        functools.partial(early_kernel, depth, rows),
        out_shape=[shifted] * LAYERS + [pltpu.VMEM((planes, LANES), F32)] * LAYERS,
        in_specs=vmem(2 + len(strips)),
        out_specs=vmem(2 * LAYERS),
        compiler_params=room(12),
        cost_estimate=pl.CostEstimate(flops=20_000_000, bytes_accessed=6_000_000, transcendentals=0),
        name="early",
    )(*(near(v) for v in (local, sibling, *strips)))
    operands = [local, sibling, outer, *strips, *corners, forward, backward, *early[LAYERS:]]
    count = len(operands)
    h_own, keep, send, *_ = pl.pallas_call(
        functools.partial(layers_kernel, depth, rows, channels, len(y_rounds), factor),
        out_shape=[
            pltpu.VMEM(((rows + 1) * planes, LANES), F32),
            pltpu.VMEM((tiles // 2, LANES), F32),
            pltpu.VMEM((tiles // 2 + 3 * planes, LANES), F32),
        ]
        + [shifted] * LAYERS,
        in_specs=vmem(count + LAYERS),
        out_specs=vmem(3 + LAYERS),
        input_output_aliases={count + k: 3 + k for k in range(LAYERS)},
        scratch_shapes=[shifted_side, shifted, shifted_side, pltpu.VMEM((tiles, LANES), F32)],
        compiler_params=room(16),
        name="layers",
    )(*(near(v) for v in operands + list(early[:LAYERS])))

    def input_gradient(swapped):
        ringed = lax.ppermute(swapped[planes:], "gx", across)
        return pl.pallas_call(
            functools.partial(grad_kernel, depth, rows, channels),
            out_shape=shape((planes * rows, cols), F32),
            in_specs=vmem(4),
            out_specs=vmem(1)[0],
            scratch_shapes=[shifted],
            compiler_params=room(8),
            cost_estimate=pl.CostEstimate(flops=600_000_000, bytes_accessed=1_000_000, transcendentals=0),
            name="grad_input",
        )(near(h_own), near(swapped), near(ringed), near(backward))

    mine, other, grad = reduce_halves(keep, send, input_gradient, gx_size, gy_size)
    results = pl.pallas_call(
        functools.partial(unpack_kernel, channels),
        out_shape=[shape(kernel_one.shape, F32)] * LAYERS,
        in_specs=vmem(2),
        out_specs=vmem(LAYERS),
        scratch_shapes=[pltpu.VMEM((tiles, LANES), F32)],
        compiler_params=room(8),
        name="unpack",
    )(near(mine), near(other))
    return (grad.reshape(input_one.shape), results[2], results[1], results[0])


def solution(mesh):
    placed = (
        P(None, None, "gx", "gy"),
        P(None, None, "gx", "gy"),
        P(None, None, "gx", "gy"),
        P(None, None, "gx", "gy"),
        P(),
        P(),
        P(),
    )
    return jax.shard_map(
        per_device,
        mesh=mesh,
        in_specs=placed,
        out_specs=(P(None, None, "gx", "gy"), P(), P(), P()),
        check_vma=False,
    )
```

```python
import functools
import math

import jax
import jax.numpy as jnp
from jax import lax
from jax.experimental import pallas as pl
from jax.experimental.pallas import tpu as pltpu
from jax.sharding import PartitionSpec as P

inv_root_two = 0.7071067811865476
inv_root_two_pi = 0.3989422804014327

LAYERS = 3
HALO = LAYERS + 1
SIDE = 2 * HALO
LANES = 128
F32 = jnp.float32
BF16 = jnp.bfloat16
NN = (((1,), (0,)), ((), ()))
NT = (((1,), (1,)), ((), ()))

WIDTHS = (LAYERS, LAYERS - 1, LAYERS - 1, LAYERS - 2)
STARTS = tuple(sum(WIDTHS[:f]) for f in range(4))
SLABS = sum(WIDTHS)


def gelu_slope(value):
    normal_cdf = 0.5 * (1.0 + lax.erf(value * inv_root_two))
    density = jnp.exp(-0.5 * value * value) * inv_root_two_pi
    return normal_cdf + value * density


def roll(value, shift):
    if not isinstance(shift, int):
        return pltpu.roll(value, lax.rem(shift + LANES, LANES), 1)
    shift %= LANES
    return pltpu.roll(value, shift, 1) if shift else value


def lane_index(rows):
    return lax.broadcasted_iota(jnp.int32, (rows, LANES), 1)


def near(value):
    return pltpu.with_memory_space_constraint(value, pltpu.VMEM)


def far(value):
    return pltpu.with_memory_space_constraint(value, pltpu.HBM)


def room(mib):
    return pltpu.CompilerParams(vmem_limit_bytes=mib * 1024 * 1024)


def vmem(count):
    return [pl.BlockSpec(memory_space=pltpu.VMEM)] * count


def slab_at(ref, field, depth, rows, row):
    size = ref.shape[0] // 4
    channels = size // (depth * rows)
    parts = [
        ref[pl.ds(field * size + z * rows + row, channels, stride=depth * rows), :] for z in range(depth)
    ]
    return jnp.concatenate(parts, axis=0)


def split(value):
    high = value.astype(BF16)
    low = (value - high.astype(F32)).astype(BF16)
    return high, low


def fetch_kernel(*refs):
    count = 4 + LAYERS
    sources, (local, *kernels), semaphores = refs[:count], refs[count : count + 1 + LAYERS], refs[-1]
    size = sources[0].shape[0]
    targets = [local.at[pl.ds(f * size, size), :] for f in range(4)] + kernels
    copies = [
        pltpu.make_async_copy(source, target, semaphores.at[k])
        for k, (source, target) in enumerate(zip(sources, targets))
    ]
    for copy in copies:
        copy.start()
    for copy in copies:
        copy.wait()


def pack_rows(depth, rows, sibling, out):
    odd = lax.rem(lax.axis_index("gx"), 2)
    planes = sibling.shape[0] // (4 * rows)
    for f, width in enumerate(WIDTHS):
        for j in range(width):
            row = (rows - width) * (1 - odd) + j
            out[pl.ds((STARTS[f] + j) * planes, planes), :] = slab_at(sibling, f, depth, rows, row)


def pack_strips(depth, rows, local, sibling, strips, strip):
    planes = local.shape[0] // (4 * rows)
    lane = lane_index(planes)
    for k, ref in enumerate((local, sibling)):
        total = jnp.zeros((planes, LANES), F32)
        for f in range(4):
            for r in range(rows):
                value = slab_at(ref, f, depth, rows, r)
                base = (f * rows + r) * SIDE
                here = (lane >= base) & (lane < base + SIDE)
                total = jnp.where(here, roll(value, base + HALO), total)
        strips[pl.ds(k * planes, planes), :] = total
    strip[...] = total


def weight_kernel(channels, depth, *refs):
    kernels, (forward, backward) = refs[:LAYERS], refs[LAYERS:]
    planes = channels * depth
    in_low = lax.rem(lane_index(channels), planes) < channels
    for layer in range(LAYERS):
        for b in range(3):
            for c in range(3):
                tiles = []
                for a in range(3):
                    tap = kernels[layer][9 * a + 3 * b + c]
                    tiles.append(jnp.concatenate([tap] * (LANES // channels), axis=1))
                upper = jnp.where(in_low, tiles[1], tiles[2])
                lower = jnp.where(in_low, tiles[0], tiles[1])
                whole = jnp.concatenate([upper, lower], axis=0)
                turned = jnp.concatenate([whole, whole], axis=0).T[:planes]
                for ref, value, bb, cc in ((forward, whole, b, c), (backward, turned, 2 - b, 2 - c)):
                    base, lanes = layer * 2 * planes, pl.ds((bb * 3 + cc) * LANES, LANES)
                    high, low = split(value)
                    ref[pl.ds(base, planes), lanes] = high
                    ref[pl.ds(base + planes, planes), lanes] = low


def conv(weights, layer, window):
    planes = weights.shape[0] // (LAYERS * 2)
    kernel = weights[pl.ds(layer * 2 * planes, 2 * planes), :]
    total = lax.dot_general(kernel, window, NN, preferred_element_type=F32)
    return total[:planes] + total[planes:]


def conv_rows(weights, layer, source, low, high):
    out = {}
    for e in range(low, high, 2):
        count = min(2, high - e)
        window = [source[:, pl.ds((e + b - 1) * LANES, count * LANES)] for b in range(3)]
        value = conv(weights, layer, jnp.concatenate(window, axis=0))
        for k in range(count):
            out[e + k] = value[:, k * LANES : (k + 1) * LANES]
    return out


def store_split(target, c, lanes, value):
    planes = value.shape[0]
    high, low = split(value)
    target[pl.ds(c * LANES, planes), lanes] = high
    target[pl.ds(c * LANES + planes, planes), lanes] = low


def shift_rows(main, side, into, edges=None):
    lane = lane_index(side.shape[0])
    for e, value in main:
        base, start = e * SIDE, e * LANES
        if not isinstance(e, int):
            start = pl.multiple_of(start, LANES)
        ends = roll(side, -base)
        down = roll(jnp.where(lane == LANES - 1, ends, value), 1)
        up = roll(jnp.where(lane == 0, ends, value), -1)
        for c, shifted in enumerate((down, value, up)):
            store_split(into, c, pl.ds(start, LANES), shifted)
        if edges is not None:
            edges = jnp.where((lane == base) | (lane == base - 1), roll(value, base), edges)
    return edges


def shift_side(side, edges, into):
    place = lax.rem(lane_index(side.shape[0]), SIDE)
    ahead = roll(jnp.where(place == 0, edges, side), -1)
    behind = roll(jnp.where(place == SIDE - 1, edges, side), 1)
    for c, shifted in enumerate((behind, side, ahead)):
        store_split(into, c, pl.ds(0, LANES), shifted)


def side_strips(got, y_odd):
    zero = jnp.zeros_like(got[0])
    got = (got + [zero])[:2]
    from_right = jnp.where(y_odd, got[1], got[0])
    from_left = jnp.where(y_odd, got[0], got[1])
    return jnp.where(lax.rem(lane_index(zero.shape[0]), SIDE) >= HALO, from_right, from_left)


def field_side(f, rows, before, own, after):
    lane = lane_index(own.shape[0])
    span, lead = rows * SIDE, HALO * SIDE - HALO
    before = roll(before, lead - span - f * span)
    after = roll(after, lead + span - f * span)
    side = jnp.where(lane < lead + span, roll(own, lead - f * span), after)
    side = jnp.where(lane < lead, before, side)
    return jnp.where(lane < lead + 2 * span, side, 0.0)


INPUTS = (0, 2, 3)


def early_kernel(depth, rows, *refs):
    local, sibling, *strips = refs[: -2 * LAYERS]
    shifted, edges = refs[-2 * LAYERS : -LAYERS], refs[-LAYERS:]
    planes = local.shape[0] // (4 * rows)
    odd = lax.rem(lax.axis_index("gx"), 2)
    y_odd = lax.rem(lax.axis_index("gy"), 2) == 1
    own, inner = (side_strips([v[pl.ds(k * planes, planes), :] for v in strips], y_odd) for k in range(2))
    for layer, f in enumerate(INPUTS):
        width = WIDTHS[f]
        side = field_side(f, rows, inner, own, inner)
        main = [(HALO + r, slab_at(local, f, depth, rows, r)) for r in range(rows)]
        for j in range(width):
            e = odd * (HALO - width) + (1 - odd) * (HALO + rows) + j
            main.append((e, slab_at(sibling, f, depth, rows, (rows - width) * odd + j)))
        zero = jnp.zeros((planes, LANES), F32)
        edges[layer][...] = shift_rows(main, side, shifted[layer], zero)


def conv_side(weights, layer, shifted):
    planes = weights.shape[0] // (LAYERS * 2)
    parts = []
    for b in range(3):
        kernel = weights[pl.ds(layer * 2 * planes, 2 * planes), pl.ds(b * 3 * LANES, 3 * LANES)]
        part = lax.dot_general(kernel, shifted[...], NN, preferred_element_type=F32)
        parts.append(roll(part[:planes] + part[planes:], -(b - 1) * SIDE))
    return parts[0] + parts[1] + parts[2]


def layers_kernel(depth, rows, channels, gy_rounds, factor, *refs):
    refs = list(refs)
    take = lambda count: [refs.pop(0) for _ in range(count)]
    local, sibling, outer = take(3)
    strips, corners = take(gy_rounds), take(gy_rounds)
    forward, backward = take(2)
    early_edges = take(LAYERS)
    take(LAYERS)
    h_out, keep, send = take(3)
    shifted = take(LAYERS)
    xside, hs, hside, gsum = refs
    planes = depth * channels
    gx, gy = lax.axis_index("gx"), lax.axis_index("gy")
    gx_size, gy_size = lax.axis_size("gx"), lax.axis_size("gy")
    x_odd, y_odd = lax.rem(gx, 2) == 1, lax.rem(gy, 2) == 1
    odd = lax.rem(gx, 2)
    ended = (gx == 0) | (gx == gx_size - 1)
    lane = lane_index(planes)

    own, inner = (side_strips([v[pl.ds(k * planes, planes), :] for v in strips], y_odd) for k in range(2))
    corner = jnp.where(ended, 0.0, side_strips([v[...] for v in corners], y_odd))
    before, after = jnp.where(x_odd, inner, corner), jnp.where(x_odd, corner, inner)

    def outer_row(f, j):
        value = outer[pl.ds((STARTS[f] + j) * planes, planes), :]
        return jnp.where(ended, 0.0, value)

    def cotangent_rows():
        f, main = 1, {}
        width = WIDTHS[f]
        for j in range(width):
            a = slab_at(sibling, f, depth, rows, (rows - width) * odd + j)
            b = outer_row(f, j)
            main[HALO - width + j] = jnp.where(x_odd, a, b)
            main[HALO + rows + j] = jnp.where(x_odd, b, a)
        for r in range(rows):
            main[HALO + r] = slab_at(local, f, depth, rows, r)
        return main

    side_row = (lane + HALO) // SIDE
    right = lax.rem(lane + HALO, SIDE) >= HALO
    row_low = jnp.where(gx > 0, 0, HALO)
    row_high = jnp.where(gx < gx_size - 1, 2 * HALO + rows, HALO + rows)
    col_ok = jnp.where(right, (gy < gy_size - 1).astype(jnp.int32), (gy > 0).astype(jnp.int32))
    side_ok = (side_row >= row_low) & (side_row < row_high) & (col_ok > 0)

    padding = gsum.shape[0] - LAYERS * 7 * channels
    if padding:
        gsum[pl.ds(LAYERS * 7 * channels, padding), :] = jnp.zeros((padding, LANES), F32)
    grad_main, grad_side = cotangent_rows(), field_side(1, rows, before, own, after)
    half = lane_index(channels)
    for layer in range(LAYERS):
        f, xs = INPUTS[layer], shifted[layer]
        x_side = field_side(f, rows, before, own, after)
        x_main = []
        for j in range(WIDTHS[f]):
            e = (1 - odd) * (HALO - WIDTHS[f]) + odd * (HALO + rows) + j
            x_main.append((e, outer_row(f, j)))
        shift_side(x_side, shift_rows(x_main, x_side, xs, early_edges[layer][...]), xside)
        h_width = LAYERS - 1 - layer
        low, high = HALO - h_width, HALO + rows + h_width
        pre = conv_rows(forward, layer, xs, low, high)
        h_main = {}
        for e in range(low, high):
            value = grad_main[e] * gelu_slope(pre[e])
            if e < HALO:
                value = jnp.where(gx > 0, value, 0.0)
            if e >= HALO + rows:
                value = jnp.where(gx < gx_size - 1, value, 0.0)
            h_main[e] = value
        h_side = jnp.where(side_ok, grad_side * gelu_slope(conv_side(forward, layer, xside)), 0.0)
        if h_width:
            edges = shift_rows(h_main.items(), h_side, hs, jnp.zeros((planes, LANES), F32))
            shift_side(h_side, edges, hside)
            center = hs[pl.ds(LANES, 2 * planes), pl.ds(HALO * LANES, rows * LANES)]
        else:
            parts = [split(h_main[HALO + r]) for r in range(rows)]
            center = [jnp.concatenate([part[k] for part in parts], axis=1) for k in range(2)]
            center = jnp.concatenate(center, axis=0)
        blocks = []
        for m in range(9):
            at = pl.ds((HALO + m // 3 - 1) * LANES, rows * LANES)
            base = m % 3 * LANES
            parts = [xs[pl.ds(base + k * planes, planes), at] for k in range(2)]
            blocks.append(jnp.concatenate(parts, axis=1))
        window = jnp.concatenate(blocks + blocks[-1:], axis=0)
        center = jnp.concatenate([center, center], axis=1)
        product = lax.dot_general(center, window, NT, preferred_element_type=F32)
        product = (product[:planes] + product[planes:]) * factor
        first = lax.rem(half // channels, 2) == 0
        mixed, summed = [], []
        for t in range(5):
            part = product[:, t * LANES : (t + 1) * LANES]
            upper, lower = part[:channels], part[channels:]
            mixed.append(jnp.where(first, lower, upper))
            summed.append(upper + roll(lower, -channels))
        tiles = mixed[:4] + [jnp.where(half < planes, mixed[4], summed[4])]
        for t in (0, 2):
            tiles.append(jnp.where(first, summed[t], roll(summed[t + 1], channels)))
        for m, tile in enumerate(tiles):
            gsum[pl.ds((layer * 7 + m) * channels, channels), :] = tile

        if h_width:
            g_width = h_width - 1
            grad_main = conv_rows(backward, layer, hs, HALO - g_width, HALO + rows + g_width)
            grad_side = conv_side(backward, layer, hside)

    for r in range(rows):
        h_out[pl.ds(r * planes, planes), :] = h_main[HALO + r]
    h_out[pl.ds(rows * planes, planes), :] = h_side
    head, tail = h_main[HALO], h_main[HALO + rows - 1]
    base = keep.shape[0]
    send[pl.ds(base, planes), :] = jnp.where(x_odd, head, tail)
    send[pl.ds(base + planes, planes), :] = jnp.where(x_odd, tail, head)
    send[pl.ds(base + 2 * planes, planes), :] = h_side
    size = keep.shape[0] // 4
    core, quad = quad_place(gx, gy)
    for k in range(4):
        piece = lax.bitwise_xor(quad, k) * size
        at = pl.ds(k * size, size)
        keep[at, :] = gsum[pl.ds(pl.multiple_of(core * 4 * size + piece, 8), size), :]
        send[at, :] = gsum[pl.ds(pl.multiple_of((1 - core) * 4 * size + piece, 8), size), :]


def quad_place(gx, gy):
    return lax.rem(gx, 2), lax.rem(gy, 2) + 2 * lax.rem(gx // 2, 2)


def grad_kernel(depth, rows, channels, own, swapped, ringed, backward, grad_out, hs):
    planes = depth * channels
    gx, gx_size = lax.axis_index("gx"), lax.axis_size("gx")
    x_odd, ended = lax.rem(gx, 2) == 1, (gx == 0) | (gx == gx_size - 1)
    lane = lane_index(planes)
    span = rows * SIDE
    inner, inner_side = swapped[pl.ds(0, planes), :], swapped[pl.ds(2 * planes, planes), :]
    outer = jnp.where(ended, 0.0, ringed[pl.ds(0, planes), :])
    outer_side = jnp.where(ended, 0.0, ringed[pl.ds(planes, planes), :])
    main = {HALO + r: own[pl.ds(r * planes, planes), :] for r in range(rows)}
    main[HALO - 1] = jnp.where(x_odd, inner, outer)
    main[HALO + rows] = jnp.where(x_odd, outer, inner)
    before = roll(jnp.where(x_odd, inner_side, outer_side), -span)
    after = roll(jnp.where(x_odd, outer_side, inner_side), span)
    side = own[pl.ds(rows * planes, planes), :]
    lead = HALO * SIDE - HALO
    side = jnp.where(lane < lead, before, jnp.where(lane < lead + span, side, after))
    shift_rows(main.items(), side, hs)
    grad_main = conv_rows(backward, LAYERS - 1, hs, HALO, HALO + rows)
    for r in range(rows):
        for z in range(depth):
            at = pl.ds(z * rows + r, channels, stride=depth * rows)
            grad_out[at, :] = grad_main[HALO + r][z * channels : (z + 1) * channels]


def unpack_kernel(channels, mine, other, *refs):
    outs, whole = refs[:LAYERS], refs[LAYERS]
    size = mine.shape[0] // 4
    core, quad = quad_place(lax.axis_index("gx"), lax.axis_index("gy"))
    for k in range(4):
        piece = lax.bitwise_xor(quad, k) * size
        at = pl.ds(k * size, size)
        whole[pl.ds(pl.multiple_of(core * 4 * size + piece, 8), size), :] = mine[at, :]
        whole[pl.ds(pl.multiple_of((1 - core) * 4 * size + piece, 8), size), :] = other[at, :]
    places = [[(s % 2 * 2, 2 * t + s // 2) for s in range(4)] for t in range(4)]
    places.append([(0, 8), (2, 8), (1, 8)])
    places += [[(1, t + k) for k in (0, 2, 1, 3)] for t in (0, 4)]
    for layer in range(LAYERS):
        for t, blocks in enumerate(places):
            tile = whole[pl.ds((layer * 7 + t) * channels, channels), :]
            for s, (a, m) in enumerate(blocks):
                outs[layer][9 * a + m] = roll(tile, -s * channels)[:, :channels]


def pair_rounds(size):
    rounds = []
    for start in range(2):
        pairs = [(i, i + 1) for i in range(start, size - 1, 2)]
        if pairs:
            rounds.append(pairs + [(j, i) for i, j in pairs])
    return rounds


def reduce_halves(keep, send, beside, gx_size, gy_size):
    axes = ("gx", "gy")
    total = gx_size * gy_size

    def swap(value, bits):
        return lax.ppermute(value, axes, [(i, i ^ bits) for i in range(total)])

    core, quad = gy_size, (1, 2 * gy_size, 2 * gy_size + 1)
    got = swap(send, core)
    count = keep.shape[0]
    value, beside = keep + got[:count], beside(got[count:])
    size = value.shape[0] // 4
    pieces = [value[k * size : (k + 1) * size] for k in range(4)]
    got = [swap(pieces[k + 1], quad[k]) for k in range(3)]
    value = (pieces[0] + got[0]) + (got[1] + got[2])
    bits = [gy_size << k for k in range(2, gx_size.bit_length() - 1)]
    bits += [1 << k for k in range(1, gy_size.bit_length() - 1)]
    while bits:
        low, *high = bits[:2]
        if high:
            got = [swap(value, b) for b in (low, high[0], low | high[0])]
            value = (value + got[0]) + (got[1] + got[2])
        else:
            value = value + swap(value, low)
        bits = bits[2:]
    value, beside = lax.optimization_barrier((value, beside))
    value = jnp.concatenate([value] + [swap(value, b) for b in quad])
    return value, swap(value, core), beside


def per_device(input_one, input_two, input_three, cotangent, kernel_one, kernel_two, kernel_three):
    channels, depth, rows, cols = input_one.shape
    gx_size, gy_size = lax.axis_size("gx"), lax.axis_size("gy")
    planes = channels * depth
    factor = 1.0 / math.sqrt(depth * rows * cols * gx_size * gy_size)
    fields = [v.reshape(planes * rows, cols) for v in (input_three, cotangent, input_two, input_one)]
    shape = jax.ShapeDtypeStruct

    kernels = [kernel_three, kernel_two, kernel_one]
    size = planes * rows
    local, *kernels = pl.pallas_call(
        fetch_kernel,
        out_shape=[pltpu.VMEM((4 * size, cols), F32)] + [pltpu.VMEM(v.shape, F32) for v in kernels],
        in_specs=[pl.BlockSpec(memory_space=pltpu.HBM)] * (4 + LAYERS),
        out_specs=vmem(1 + LAYERS),
        scratch_shapes=[pltpu.SemaphoreType.DMA((4 + LAYERS,))],
        compiler_params=room(8),
        name="fetch",
    )(*(far(v) for v in fields + kernels))

    sibling = lax.ppermute(local, "gx", [(i, i ^ 1) for i in range(gx_size)])
    across = [(i, i - 2) if i % 2 else (i, i + 2) for i in range(gx_size)]
    across = [(i, j) if 0 <= j < gx_size else (i, i ^ 1) for i, j in across]
    y_rounds = pair_rounds(gy_size)
    weight_shape = pltpu.VMEM((LAYERS * 2 * planes, 9 * LANES), BF16)
    forward, backward = pl.pallas_call(
        functools.partial(weight_kernel, channels, depth),
        out_shape=[weight_shape, weight_shape],
        in_specs=vmem(LAYERS),
        out_specs=vmem(2),
        cost_estimate=pl.CostEstimate(flops=20_000_000, bytes_accessed=4_000_000, transcendentals=0),
        compiler_params=room(12),
        name="weights",
    )(*(near(v) for v in kernels))

    sibling, forward, backward = lax.optimization_barrier((sibling, forward, backward))
    outer = pl.pallas_call(
        functools.partial(pack_rows, depth, rows),
        out_shape=pltpu.VMEM((SLABS * planes, cols), F32),
        in_specs=vmem(1),
        out_specs=vmem(1)[0],
        compiler_params=room(8),
        name="pack_rows",
    )(near(sibling))
    strips, strip = pl.pallas_call(
        functools.partial(pack_strips, depth, rows),
        out_shape=[pltpu.VMEM((2 * planes, cols), F32), pltpu.VMEM((planes, cols), F32)],
        in_specs=vmem(2),
        out_specs=vmem(2),
        compiler_params=room(8),
        cost_estimate=pl.CostEstimate(flops=5_000_000, bytes_accessed=2_000_000, transcendentals=0),
        name="pack_strips",
    )(near(local), near(sibling))

    def diagonal(x_pairs, y_pairs):
        return [(i * gy_size + k, j * gy_size + m) for i, j in x_pairs for k, m in y_pairs]

    outer = lax.ppermute(outer, "gx", across)
    corners = [lax.ppermute(strip, ("gx", "gy"), diagonal(across, pairs)) for pairs in y_rounds]
    strips = [lax.ppermute(strips, "gy", pairs) for pairs in y_rounds]

    tiles = -(-LAYERS * 7 * channels // 64) * 64
    span = (2 * HALO + rows) * LANES
    shifted, shifted_side = pltpu.VMEM((3 * LANES, span), BF16), pltpu.VMEM((3 * LANES, LANES), BF16)
    early = pl.pallas_call(
        functools.partial(early_kernel, depth, rows),
        out_shape=[shifted] * LAYERS + [pltpu.VMEM((planes, LANES), F32)] * LAYERS,
        in_specs=vmem(2 + len(strips)),
        out_specs=vmem(2 * LAYERS),
        compiler_params=room(12),
        cost_estimate=pl.CostEstimate(flops=20_000_000, bytes_accessed=6_000_000, transcendentals=0),
        name="early",
    )(*(near(v) for v in (local, sibling, *strips)))
    operands = [local, sibling, outer, *strips, *corners, forward, backward, *early[LAYERS:]]
    count = len(operands)
    h_own, keep, send, *_ = pl.pallas_call(
        functools.partial(layers_kernel, depth, rows, channels, len(y_rounds), factor),
        out_shape=[
            pltpu.VMEM(((rows + 1) * planes, LANES), F32),
            pltpu.VMEM((tiles // 2, LANES), F32),
            pltpu.VMEM((tiles // 2 + 3 * planes, LANES), F32),
        ]
        + [shifted] * LAYERS,
        in_specs=vmem(count + LAYERS),
        out_specs=vmem(3 + LAYERS),
        input_output_aliases={count + k: 3 + k for k in range(LAYERS)},
        scratch_shapes=[shifted_side, shifted, shifted_side, pltpu.VMEM((tiles, LANES), F32)],
        compiler_params=room(16),
        name="layers",
    )(*(near(v) for v in operands + list(early[:LAYERS])))

    def input_gradient(swapped):
        ringed = lax.ppermute(swapped[planes:], "gx", across)
        return pl.pallas_call(
            functools.partial(grad_kernel, depth, rows, channels),
            out_shape=shape((planes * rows, cols), F32),
            in_specs=vmem(4),
            out_specs=vmem(1)[0],
            scratch_shapes=[shifted],
            compiler_params=room(8),
            cost_estimate=pl.CostEstimate(flops=600_000_000, bytes_accessed=1_000_000, transcendentals=0),
            name="grad_input",
        )(near(h_own), near(swapped), near(ringed), near(backward))

    mine, other, grad = reduce_halves(keep, send, input_gradient, gx_size, gy_size)
    results = pl.pallas_call(
        functools.partial(unpack_kernel, channels),
        out_shape=[shape(kernel_one.shape, F32)] * LAYERS,
        in_specs=vmem(2),
        out_specs=vmem(LAYERS),
        scratch_shapes=[pltpu.VMEM((tiles, LANES), F32)],
        compiler_params=room(8),
        name="unpack",
    )(near(mine), near(other))
    return (grad.reshape(input_one.shape), results[2], results[1], results[0])


def solution(mesh):
    placed = (
        P(None, None, "gx", "gy"),
        P(None, None, "gx", "gy"),
        P(None, None, "gx", "gy"),
        P(None, None, "gx", "gy"),
        P(),
        P(),
        P(),
    )
    return jax.shard_map(
        per_device,
        mesh=mesh,
        in_specs=placed,
        out_specs=(P(None, None, "gx", "gy"), P(), P(), P()),
        check_vma=False,
    )
```

```python
import functools
import math

import jax
import jax.numpy as jnp
from jax import lax
from jax.experimental import pallas as pl
from jax.experimental.pallas import tpu as pltpu
from jax.sharding import PartitionSpec as P

inv_root_two = 0.7071067811865476
inv_root_two_pi = 0.3989422804014327

LAYERS = 3
HALO = LAYERS + 1
SIDE = 2 * HALO
LANES = 128
F32 = jnp.float32
BF16 = jnp.bfloat16
NN = (((1,), (0,)), ((), ()))
NT = (((1,), (1,)), ((), ()))

WIDTHS = (LAYERS, LAYERS - 1, LAYERS - 1, LAYERS - 2)
STARTS = tuple(sum(WIDTHS[:f]) for f in range(4))
SLABS = sum(WIDTHS)


def gelu_slope(value):
    normal_cdf = 0.5 * (1.0 + lax.erf(value * inv_root_two))
    density = jnp.exp(-0.5 * value * value) * inv_root_two_pi
    return normal_cdf + value * density


def roll(value, shift):
    if not isinstance(shift, int):
        return pltpu.roll(value, lax.rem(shift + LANES, LANES), 1)
    shift %= LANES
    return pltpu.roll(value, shift, 1) if shift else value


def lane_index(rows):
    return lax.broadcasted_iota(jnp.int32, (rows, LANES), 1)


def near(value):
    return pltpu.with_memory_space_constraint(value, pltpu.VMEM)


def far(value):
    return pltpu.with_memory_space_constraint(value, pltpu.HBM)


def room(mib):
    return pltpu.CompilerParams(vmem_limit_bytes=mib * 1024 * 1024)


def vmem(count):
    return [pl.BlockSpec(memory_space=pltpu.VMEM)] * count


def slab_at(ref, field, depth, rows, row):
    size = ref.shape[0] // 4
    channels = size // (depth * rows)
    parts = [
        ref[pl.ds(field * size + z * rows + row, channels, stride=depth * rows), :] for z in range(depth)
    ]
    return jnp.concatenate(parts, axis=0)


def split(value):
    high = value.astype(BF16)
    low = (value - high.astype(F32)).astype(BF16)
    return high, low


def run_copies(sources, targets, semaphores):
    copies = [
        pltpu.make_async_copy(source, target, semaphores.at[k])
        for k, (source, target) in enumerate(zip(sources, targets))
    ]
    for copy in copies:
        copy.start()
    for copy in copies:
        copy.wait()


def fetch_fields(*refs):
    sources, local, semaphores = refs[:4], refs[4], refs[5]
    size = sources[0].shape[0]
    run_copies(sources, [local.at[pl.ds(f * size, size), :] for f in range(4)], semaphores)


def fetch_kernels(*refs):
    run_copies(refs[:LAYERS], refs[LAYERS:-1], refs[-1])


def pack_rows(depth, rows, sibling, out):
    odd = lax.rem(lax.axis_index("gx"), 2)
    planes = sibling.shape[0] // (4 * rows)
    for f, width in enumerate(WIDTHS):
        for j in range(width):
            row = (rows - width) * (1 - odd) + j
            out[pl.ds((STARTS[f] + j) * planes, planes), :] = slab_at(sibling, f, depth, rows, row)


def pack_strips(depth, rows, local, sibling, strips, strip):
    planes = local.shape[0] // (4 * rows)
    lane = lane_index(planes)
    for k, ref in enumerate((local, sibling)):
        total = jnp.zeros((planes, LANES), F32)
        for f in range(4):
            for r in range(rows):
                value = slab_at(ref, f, depth, rows, r)
                base = (f * rows + r) * SIDE
                here = (lane >= base) & (lane < base + SIDE)
                total = jnp.where(here, roll(value, base + HALO), total)
        strips[pl.ds(k * planes, planes), :] = total
    strip[...] = total


def weight_kernel(channels, depth, *refs):
    kernels, (forward, backward) = refs[:LAYERS], refs[LAYERS:]
    planes = channels * depth
    in_low = lax.rem(lane_index(channels), planes) < channels
    for layer in range(LAYERS):
        for b in range(3):
            for c in range(3):
                tiles = []
                for a in range(3):
                    tap = kernels[layer][9 * a + 3 * b + c]
                    tiles.append(jnp.concatenate([tap] * (LANES // channels), axis=1))
                upper = jnp.where(in_low, tiles[1], tiles[2])
                lower = jnp.where(in_low, tiles[0], tiles[1])
                whole = jnp.concatenate([upper, lower], axis=0)
                turned = jnp.concatenate([whole, whole], axis=0).T[:planes]
                for ref, value, bb, cc in ((forward, whole, b, c), (backward, turned, 2 - b, 2 - c)):
                    base, lanes = layer * 2 * planes, pl.ds((bb * 3 + cc) * LANES, LANES)
                    high, low = split(value)
                    ref[pl.ds(base, planes), lanes] = high
                    ref[pl.ds(base + planes, planes), lanes] = low


def conv(weights, layer, window):
    planes = weights.shape[0] // (LAYERS * 2)
    kernel = weights[pl.ds(layer * 2 * planes, 2 * planes), :]
    total = lax.dot_general(kernel, window, NN, preferred_element_type=F32)
    return total[:planes] + total[planes:]


def conv_rows(weights, layer, source, low, high):
    out = {}
    for e in range(low, high, 2):
        count = min(2, high - e)
        window = [source[:, pl.ds((e + b - 1) * LANES, count * LANES)] for b in range(3)]
        value = conv(weights, layer, jnp.concatenate(window, axis=0))
        for k in range(count):
            out[e + k] = value[:, k * LANES : (k + 1) * LANES]
    return out


def store_split(target, c, lanes, value):
    planes = value.shape[0]
    high, low = split(value)
    target[pl.ds(c * LANES, planes), lanes] = high
    target[pl.ds(c * LANES + planes, planes), lanes] = low


def shift_rows(main, side, into, edges=None):
    lane = lane_index(side.shape[0])
    for e, value in main:
        base, start = e * SIDE, e * LANES
        if not isinstance(e, int):
            start = pl.multiple_of(start, LANES)
        ends = roll(side, -base)
        down = roll(jnp.where(lane == LANES - 1, ends, value), 1)
        up = roll(jnp.where(lane == 0, ends, value), -1)
        for c, shifted in enumerate((down, value, up)):
            store_split(into, c, pl.ds(start, LANES), shifted)
        if edges is not None:
            edges = jnp.where((lane == base) | (lane == base - 1), roll(value, base), edges)
    return edges


def shift_side(side, edges, into):
    place = lax.rem(lane_index(side.shape[0]), SIDE)
    ahead = roll(jnp.where(place == 0, edges, side), -1)
    behind = roll(jnp.where(place == SIDE - 1, edges, side), 1)
    for c, shifted in enumerate((behind, side, ahead)):
        store_split(into, c, pl.ds(0, LANES), shifted)


def side_strips(got, y_odd):
    zero = jnp.zeros_like(got[0])
    got = (got + [zero])[:2]
    from_right = jnp.where(y_odd, got[1], got[0])
    from_left = jnp.where(y_odd, got[0], got[1])
    return jnp.where(lax.rem(lane_index(zero.shape[0]), SIDE) >= HALO, from_right, from_left)


def field_side(f, rows, before, own, after):
    lane = lane_index(own.shape[0])
    span, lead = rows * SIDE, HALO * SIDE - HALO
    before = roll(before, lead - span - f * span)
    after = roll(after, lead + span - f * span)
    side = jnp.where(lane < lead + span, roll(own, lead - f * span), after)
    side = jnp.where(lane < lead, before, side)
    return jnp.where(lane < lead + 2 * span, side, 0.0)


INPUTS = (0, 2, 3)


def early_kernel(depth, rows, *refs):
    local, sibling, *strips = refs[: -2 * LAYERS]
    shifted, edges = refs[-2 * LAYERS : -LAYERS], refs[-LAYERS:]
    planes = local.shape[0] // (4 * rows)
    odd = lax.rem(lax.axis_index("gx"), 2)
    y_odd = lax.rem(lax.axis_index("gy"), 2) == 1
    own, inner = (side_strips([v[pl.ds(k * planes, planes), :] for v in strips], y_odd) for k in range(2))
    for layer, f in enumerate(INPUTS):
        width = WIDTHS[f]
        side = field_side(f, rows, inner, own, inner)
        main = [(HALO + r, slab_at(local, f, depth, rows, r)) for r in range(rows)]
        for j in range(width):
            e = odd * (HALO - width) + (1 - odd) * (HALO + rows) + j
            main.append((e, slab_at(sibling, f, depth, rows, (rows - width) * odd + j)))
        zero = jnp.zeros((planes, LANES), F32)
        edges[layer][...] = shift_rows(main, side, shifted[layer], zero)


def conv_side(weights, layer, shifted):
    planes = weights.shape[0] // (LAYERS * 2)
    parts = []
    for b in range(3):
        kernel = weights[pl.ds(layer * 2 * planes, 2 * planes), pl.ds(b * 3 * LANES, 3 * LANES)]
        part = lax.dot_general(kernel, shifted[...], NN, preferred_element_type=F32)
        parts.append(roll(part[:planes] + part[planes:], -(b - 1) * SIDE))
    return parts[0] + parts[1] + parts[2]


def layers_kernel(depth, rows, channels, gy_rounds, factor, *refs):
    refs = list(refs)
    take = lambda count: [refs.pop(0) for _ in range(count)]
    local, sibling, outer = take(3)
    strips, corners = take(gy_rounds), take(gy_rounds)
    forward, backward = take(2)
    early_edges = take(LAYERS)
    take(LAYERS)
    h_out, keep, send = take(3)
    shifted = take(LAYERS)
    xside, hs, hside, gsum = refs
    planes = depth * channels
    gx, gy = lax.axis_index("gx"), lax.axis_index("gy")
    gx_size, gy_size = lax.axis_size("gx"), lax.axis_size("gy")
    x_odd, y_odd = lax.rem(gx, 2) == 1, lax.rem(gy, 2) == 1
    odd = lax.rem(gx, 2)
    ended = (gx == 0) | (gx == gx_size - 1)
    lane = lane_index(planes)

    own, inner = (side_strips([v[pl.ds(k * planes, planes), :] for v in strips], y_odd) for k in range(2))
    corner = jnp.where(ended, 0.0, side_strips([v[...] for v in corners], y_odd))
    before, after = jnp.where(x_odd, inner, corner), jnp.where(x_odd, corner, inner)

    def outer_row(f, j):
        value = outer[pl.ds((STARTS[f] + j) * planes, planes), :]
        return jnp.where(ended, 0.0, value)

    def cotangent_rows():
        f, main = 1, {}
        width = WIDTHS[f]
        for j in range(width):
            a = slab_at(sibling, f, depth, rows, (rows - width) * odd + j)
            b = outer_row(f, j)
            main[HALO - width + j] = jnp.where(x_odd, a, b)
            main[HALO + rows + j] = jnp.where(x_odd, b, a)
        for r in range(rows):
            main[HALO + r] = slab_at(local, f, depth, rows, r)
        return main

    side_row = (lane + HALO) // SIDE
    right = lax.rem(lane + HALO, SIDE) >= HALO
    row_low = jnp.where(gx > 0, 0, HALO)
    row_high = jnp.where(gx < gx_size - 1, 2 * HALO + rows, HALO + rows)
    col_ok = jnp.where(right, (gy < gy_size - 1).astype(jnp.int32), (gy > 0).astype(jnp.int32))
    side_ok = (side_row >= row_low) & (side_row < row_high) & (col_ok > 0)

    padding = gsum.shape[0] - LAYERS * 7 * channels
    if padding:
        gsum[pl.ds(LAYERS * 7 * channels, padding), :] = jnp.zeros((padding, LANES), F32)
    grad_main, grad_side = cotangent_rows(), field_side(1, rows, before, own, after)
    half = lane_index(channels)
    for layer in range(LAYERS):
        f, xs = INPUTS[layer], shifted[layer]
        x_side = field_side(f, rows, before, own, after)
        x_main = []
        for j in range(WIDTHS[f]):
            e = (1 - odd) * (HALO - WIDTHS[f]) + odd * (HALO + rows) + j
            x_main.append((e, outer_row(f, j)))
        shift_side(x_side, shift_rows(x_main, x_side, xs, early_edges[layer][...]), xside)
        h_width = LAYERS - 1 - layer
        low, high = HALO - h_width, HALO + rows + h_width
        pre = conv_rows(forward, layer, xs, low, high)
        h_main = {}
        for e in range(low, high):
            value = grad_main[e] * gelu_slope(pre[e])
            if e < HALO:
                value = jnp.where(gx > 0, value, 0.0)
            if e >= HALO + rows:
                value = jnp.where(gx < gx_size - 1, value, 0.0)
            h_main[e] = value
        h_side = jnp.where(side_ok, grad_side * gelu_slope(conv_side(forward, layer, xside)), 0.0)
        if h_width:
            edges = shift_rows(h_main.items(), h_side, hs, jnp.zeros((planes, LANES), F32))
            shift_side(h_side, edges, hside)
            center = hs[pl.ds(LANES, 2 * planes), pl.ds(HALO * LANES, rows * LANES)]
        else:
            parts = [split(h_main[HALO + r]) for r in range(rows)]
            center = [jnp.concatenate([part[k] for part in parts], axis=1) for k in range(2)]
            center = jnp.concatenate(center, axis=0)
        blocks = []
        for m in range(9):
            at = pl.ds((HALO + m // 3 - 1) * LANES, rows * LANES)
            base = m % 3 * LANES
            parts = [xs[pl.ds(base + k * planes, planes), at] for k in range(2)]
            blocks.append(jnp.concatenate(parts, axis=1))
        window = jnp.concatenate(blocks + blocks[-1:], axis=0)
        center = jnp.concatenate([center, center], axis=1)
        product = lax.dot_general(center, window, NT, preferred_element_type=F32)
        product = (product[:planes] + product[planes:]) * factor
        first = lax.rem(half // channels, 2) == 0
        mixed, summed = [], []
        for t in range(5):
            part = product[:, t * LANES : (t + 1) * LANES]
            upper, lower = part[:channels], part[channels:]
            mixed.append(jnp.where(first, lower, upper))
            summed.append(upper + roll(lower, -channels))
        tiles = mixed[:4] + [jnp.where(half < planes, mixed[4], summed[4])]
        for t in (0, 2):
            tiles.append(jnp.where(first, summed[t], roll(summed[t + 1], channels)))
        for m, tile in enumerate(tiles):
            gsum[pl.ds((layer * 7 + m) * channels, channels), :] = tile

        if h_width:
            g_width = h_width - 1
            grad_main = conv_rows(backward, layer, hs, HALO - g_width, HALO + rows + g_width)
            grad_side = conv_side(backward, layer, hside)

    for r in range(rows):
        h_out[pl.ds(r * planes, planes), :] = h_main[HALO + r]
    h_out[pl.ds(rows * planes, planes), :] = h_side
    head, tail = h_main[HALO], h_main[HALO + rows - 1]
    base = keep.shape[0]
    send[pl.ds(base, planes), :] = jnp.where(x_odd, head, tail)
    send[pl.ds(base + planes, planes), :] = jnp.where(x_odd, tail, head)
    send[pl.ds(base + 2 * planes, planes), :] = h_side
    size = keep.shape[0] // 4
    core, quad = quad_place(gx, gy)
    for k in range(4):
        piece = lax.bitwise_xor(quad, k) * size
        at = pl.ds(k * size, size)
        keep[at, :] = gsum[pl.ds(pl.multiple_of(core * 4 * size + piece, 8), size), :]
        send[at, :] = gsum[pl.ds(pl.multiple_of((1 - core) * 4 * size + piece, 8), size), :]


def quad_place(gx, gy):
    return lax.rem(gx, 2), lax.rem(gy, 2) + 2 * lax.rem(gx // 2, 2)


def grad_kernel(depth, rows, channels, own, swapped, ringed, backward, grad_out, hs):
    planes = depth * channels
    gx, gx_size = lax.axis_index("gx"), lax.axis_size("gx")
    x_odd, ended = lax.rem(gx, 2) == 1, (gx == 0) | (gx == gx_size - 1)
    lane = lane_index(planes)
    span = rows * SIDE
    inner, inner_side = swapped[pl.ds(0, planes), :], swapped[pl.ds(2 * planes, planes), :]
    outer = jnp.where(ended, 0.0, ringed[pl.ds(0, planes), :])
    outer_side = jnp.where(ended, 0.0, ringed[pl.ds(planes, planes), :])
    main = {HALO + r: own[pl.ds(r * planes, planes), :] for r in range(rows)}
    main[HALO - 1] = jnp.where(x_odd, inner, outer)
    main[HALO + rows] = jnp.where(x_odd, outer, inner)
    before = roll(jnp.where(x_odd, inner_side, outer_side), -span)
    after = roll(jnp.where(x_odd, outer_side, inner_side), span)
    side = own[pl.ds(rows * planes, planes), :]
    lead = HALO * SIDE - HALO
    side = jnp.where(lane < lead, before, jnp.where(lane < lead + span, side, after))
    shift_rows(main.items(), side, hs)
    grad_main = conv_rows(backward, LAYERS - 1, hs, HALO, HALO + rows)
    for r in range(rows):
        for z in range(depth):
            at = pl.ds(z * rows + r, channels, stride=depth * rows)
            grad_out[at, :] = grad_main[HALO + r][z * channels : (z + 1) * channels]


def unpack_kernel(channels, mine, other, *refs):
    outs, whole = refs[:LAYERS], refs[LAYERS]
    size = mine.shape[0] // 4
    core, quad = quad_place(lax.axis_index("gx"), lax.axis_index("gy"))
    for k in range(4):
        piece = lax.bitwise_xor(quad, k) * size
        at = pl.ds(k * size, size)
        whole[pl.ds(pl.multiple_of(core * 4 * size + piece, 8), size), :] = mine[at, :]
        whole[pl.ds(pl.multiple_of((1 - core) * 4 * size + piece, 8), size), :] = other[at, :]
    places = [[(s % 2 * 2, 2 * t + s // 2) for s in range(4)] for t in range(4)]
    places.append([(0, 8), (2, 8), (1, 8)])
    places += [[(1, t + k) for k in (0, 2, 1, 3)] for t in (0, 4)]
    for layer in range(LAYERS):
        for t, blocks in enumerate(places):
            tile = whole[pl.ds((layer * 7 + t) * channels, channels), :]
            for s, (a, m) in enumerate(blocks):
                outs[layer][9 * a + m] = roll(tile, -s * channels)[:, :channels]


def pair_rounds(size):
    rounds = []
    for start in range(2):
        pairs = [(i, i + 1) for i in range(start, size - 1, 2)]
        if pairs:
            rounds.append(pairs + [(j, i) for i, j in pairs])
    return rounds


def reduce_halves(keep, send, beside, gx_size, gy_size):
    axes = ("gx", "gy")
    total = gx_size * gy_size

    def swap(value, bits):
        return lax.ppermute(value, axes, [(i, i ^ bits) for i in range(total)])

    core, quad = gy_size, (1, 2 * gy_size, 2 * gy_size + 1)
    got = swap(send, core)
    count = keep.shape[0]
    value, beside = keep + got[:count], beside(got[count:])
    size = value.shape[0] // 4
    pieces = [value[k * size : (k + 1) * size] for k in range(4)]
    got = [swap(pieces[k + 1], quad[k]) for k in range(3)]
    value = (pieces[0] + got[0]) + (got[1] + got[2])
    bits = [gy_size << k for k in range(2, gx_size.bit_length() - 1)]
    bits += [1 << k for k in range(1, gy_size.bit_length() - 1)]
    while bits:
        low, *high = bits[:2]
        if high:
            got = [swap(value, b) for b in (low, high[0], low | high[0])]
            value = (value + got[0]) + (got[1] + got[2])
        else:
            value = value + swap(value, low)
        bits = bits[2:]
    value, beside = lax.optimization_barrier((value, beside))
    value = jnp.concatenate([value] + [swap(value, b) for b in quad])
    return value, swap(value, core), beside


def per_device(input_one, input_two, input_three, cotangent, kernel_one, kernel_two, kernel_three):
    channels, depth, rows, cols = input_one.shape
    gx_size, gy_size = lax.axis_size("gx"), lax.axis_size("gy")
    planes = channels * depth
    factor = 1.0 / math.sqrt(depth * rows * cols * gx_size * gy_size)
    fields = [v.reshape(planes * rows, cols) for v in (input_three, cotangent, input_two, input_one)]
    shape = jax.ShapeDtypeStruct

    kernels = [kernel_three, kernel_two, kernel_one]
    size = planes * rows
    local = pl.pallas_call(
        fetch_fields,
        out_shape=pltpu.VMEM((4 * size, cols), F32),
        in_specs=[pl.BlockSpec(memory_space=pltpu.HBM)] * 4,
        out_specs=vmem(1)[0],
        scratch_shapes=[pltpu.SemaphoreType.DMA((4,))],
        compiler_params=room(8),
        name="fetch",
    )(*(far(v) for v in fields))

    sibling = lax.ppermute(local, "gx", [(i, i ^ 1) for i in range(gx_size)])
    kernels = pl.pallas_call(
        fetch_kernels,
        out_shape=[pltpu.VMEM(v.shape, F32) for v in kernels],
        in_specs=[pl.BlockSpec(memory_space=pltpu.HBM)] * LAYERS,
        out_specs=vmem(LAYERS),
        scratch_shapes=[pltpu.SemaphoreType.DMA((LAYERS,))],
        compiler_params=room(8),
        cost_estimate=pl.CostEstimate(flops=0, bytes_accessed=4_000_000, transcendentals=0),
        name="fetch_kernels",
    )(*(far(v) for v in kernels))
    sibling, *kernels = lax.optimization_barrier((sibling, *kernels))
    across = [(i, i - 2) if i % 2 else (i, i + 2) for i in range(gx_size)]
    across = [(i, j) if 0 <= j < gx_size else (i, i ^ 1) for i, j in across]
    y_rounds = pair_rounds(gy_size)
    outer = pl.pallas_call(
        functools.partial(pack_rows, depth, rows),
        out_shape=pltpu.VMEM((SLABS * planes, cols), F32),
        in_specs=vmem(1),
        out_specs=vmem(1)[0],
        compiler_params=room(8),
        name="pack_rows",
    )(near(sibling))
    strips, strip = pl.pallas_call(
        functools.partial(pack_strips, depth, rows),
        out_shape=[pltpu.VMEM((2 * planes, cols), F32), pltpu.VMEM((planes, cols), F32)],
        in_specs=vmem(2),
        out_specs=vmem(2),
        compiler_params=room(8),
        cost_estimate=pl.CostEstimate(flops=5_000_000, bytes_accessed=2_000_000, transcendentals=0),
        name="pack_strips",
    )(near(local), near(sibling))

    strips, *kernels = lax.optimization_barrier((strips, *kernels))
    weight_shape = pltpu.VMEM((LAYERS * 2 * planes, 9 * LANES), BF16)
    forward, backward = pl.pallas_call(
        functools.partial(weight_kernel, channels, depth),
        out_shape=[weight_shape, weight_shape],
        in_specs=vmem(LAYERS),
        out_specs=vmem(2),
        cost_estimate=pl.CostEstimate(flops=20_000_000, bytes_accessed=4_000_000, transcendentals=0),
        compiler_params=room(12),
        name="weights",
    )(*(near(v) for v in kernels))

    def diagonal(x_pairs, y_pairs):
        return [(i * gy_size + k, j * gy_size + m) for i, j in x_pairs for k, m in y_pairs]

    outer = lax.ppermute(outer, "gx", across)
    corners = [lax.ppermute(strip, ("gx", "gy"), diagonal(across, pairs)) for pairs in y_rounds]
    strips = [lax.ppermute(strips, "gy", pairs) for pairs in y_rounds]

    tiles = -(-LAYERS * 7 * channels // 64) * 64
    span = (2 * HALO + rows) * LANES
    shifted, shifted_side = pltpu.VMEM((3 * LANES, span), BF16), pltpu.VMEM((3 * LANES, LANES), BF16)
    early = pl.pallas_call(
        functools.partial(early_kernel, depth, rows),
        out_shape=[shifted] * LAYERS + [pltpu.VMEM((planes, LANES), F32)] * LAYERS,
        in_specs=vmem(2 + len(strips)),
        out_specs=vmem(2 * LAYERS),
        compiler_params=room(12),
        cost_estimate=pl.CostEstimate(flops=20_000_000, bytes_accessed=6_000_000, transcendentals=0),
        name="early",
    )(*(near(v) for v in (local, sibling, *strips)))
    operands = [local, sibling, outer, *strips, *corners, forward, backward, *early[LAYERS:]]
    count = len(operands)
    h_own, keep, send, *_ = pl.pallas_call(
        functools.partial(layers_kernel, depth, rows, channels, len(y_rounds), factor),
        out_shape=[
            pltpu.VMEM(((rows + 1) * planes, LANES), F32),
            pltpu.VMEM((tiles // 2, LANES), F32),
            pltpu.VMEM((tiles // 2 + 3 * planes, LANES), F32),
        ]
        + [shifted] * LAYERS,
        in_specs=vmem(count + LAYERS),
        out_specs=vmem(3 + LAYERS),
        input_output_aliases={count + k: 3 + k for k in range(LAYERS)},
        scratch_shapes=[shifted_side, shifted, shifted_side, pltpu.VMEM((tiles, LANES), F32)],
        compiler_params=room(16),
        name="layers",
    )(*(near(v) for v in operands + list(early[:LAYERS])))

    def input_gradient(swapped):
        ringed = lax.ppermute(swapped[planes:], "gx", across)
        return pl.pallas_call(
            functools.partial(grad_kernel, depth, rows, channels),
            out_shape=shape((planes * rows, cols), F32),
            in_specs=vmem(4),
            out_specs=vmem(1)[0],
            scratch_shapes=[shifted],
            compiler_params=room(8),
            cost_estimate=pl.CostEstimate(flops=600_000_000, bytes_accessed=1_000_000, transcendentals=0),
            name="grad_input",
        )(near(h_own), near(swapped), near(ringed), near(backward))

    mine, other, grad = reduce_halves(keep, send, input_gradient, gx_size, gy_size)
    results = pl.pallas_call(
        functools.partial(unpack_kernel, channels),
        out_shape=[shape(kernel_one.shape, F32)] * LAYERS,
        in_specs=vmem(2),
        out_specs=vmem(LAYERS),
        scratch_shapes=[pltpu.VMEM((tiles, LANES), F32)],
        compiler_params=room(8),
        name="unpack",
    )(near(mine), near(other))
    return (grad.reshape(input_one.shape), results[2], results[1], results[0])


def solution(mesh):
    placed = (
        P(None, None, "gx", "gy"),
        P(None, None, "gx", "gy"),
        P(None, None, "gx", "gy"),
        P(None, None, "gx", "gy"),
        P(),
        P(),
        P(),
    )
    return jax.shard_map(
        per_device,
        mesh=mesh,
        in_specs=placed,
        out_specs=(P(None, None, "gx", "gy"), P(), P(), P()),
        check_vma=False,
    )
```

```python
import functools
import math

import jax
import jax.numpy as jnp
from jax import lax
from jax.experimental import pallas as pl
from jax.experimental.pallas import tpu as pltpu
from jax.sharding import PartitionSpec as P

inv_root_two = 0.7071067811865476
inv_root_two_pi = 0.3989422804014327

LAYERS = 3
HALO = LAYERS + 1
SIDE = 2 * HALO
LANES = 128
F32 = jnp.float32
BF16 = jnp.bfloat16
NN = (((1,), (0,)), ((), ()))
NT = (((1,), (1,)), ((), ()))

WIDTHS = (LAYERS, LAYERS - 1, LAYERS - 1, LAYERS - 2)
STARTS = tuple(sum(WIDTHS[:f]) for f in range(4))
SLABS = sum(WIDTHS)


def gelu_slope(value):
    normal_cdf = 0.5 * (1.0 + lax.erf(value * inv_root_two))
    density = jnp.exp(-0.5 * value * value) * inv_root_two_pi
    return normal_cdf + value * density


def roll(value, shift):
    if not isinstance(shift, int):
        return pltpu.roll(value, lax.rem(shift + LANES, LANES), 1)
    shift %= LANES
    return pltpu.roll(value, shift, 1) if shift else value


def lane_index(rows):
    return lax.broadcasted_iota(jnp.int32, (rows, LANES), 1)


def near(value):
    return pltpu.with_memory_space_constraint(value, pltpu.VMEM)


def far(value):
    return pltpu.with_memory_space_constraint(value, pltpu.HBM)


def room(mib):
    return pltpu.CompilerParams(vmem_limit_bytes=mib * 1024 * 1024)


def vmem(count):
    return [pl.BlockSpec(memory_space=pltpu.VMEM)] * count


def slab_at(ref, field, depth, rows, row):
    size = ref.shape[0] // 4
    channels = size // (depth * rows)
    parts = [
        ref[pl.ds(field * size + z * rows + row, channels, stride=depth * rows), :] for z in range(depth)
    ]
    return jnp.concatenate(parts, axis=0)


def split(value):
    high = value.astype(BF16)
    low = (value - high.astype(F32)).astype(BF16)
    return high, low


def run_copies(sources, targets, semaphores):
    copies = [
        pltpu.make_async_copy(source, target, semaphores.at[k])
        for k, (source, target) in enumerate(zip(sources, targets))
    ]
    for copy in copies:
        copy.start()
    for copy in copies:
        copy.wait()


def fetch_fields(*refs):
    sources, local, semaphores = refs[:4], refs[4], refs[5]
    size = sources[0].shape[0]
    run_copies(sources, [local.at[pl.ds(f * size, size), :] for f in range(4)], semaphores)


def fetch_kernels(*refs):
    run_copies(refs[:LAYERS], refs[LAYERS:-1], refs[-1])


def pack_rows(depth, rows, sibling, out):
    odd = lax.rem(lax.axis_index("gx"), 2)
    planes = sibling.shape[0] // (4 * rows)
    for f, width in enumerate(WIDTHS):
        for j in range(width):
            row = (rows - width) * (1 - odd) + j
            out[pl.ds((STARTS[f] + j) * planes, planes), :] = slab_at(sibling, f, depth, rows, row)


def pack_strips(depth, rows, local, sibling, strips, strip):
    planes = local.shape[0] // (4 * rows)
    lane = lane_index(planes)
    for k, ref in enumerate((local, sibling)):
        total = jnp.zeros((planes, LANES), F32)
        for f in range(4):
            for r in range(rows):
                value = slab_at(ref, f, depth, rows, r)
                base = (f * rows + r) * SIDE
                here = (lane >= base) & (lane < base + SIDE)
                total = jnp.where(here, roll(value, base + HALO), total)
        strips[pl.ds(k * planes, planes), :] = total
    strip[...] = total


def weight_kernel(channels, depth, *refs):
    kernels, (forward, backward) = refs[:LAYERS], refs[LAYERS:]
    planes = channels * depth
    in_low = lax.rem(lane_index(channels), planes) < channels
    for layer in range(LAYERS):
        for b in range(3):
            for c in range(3):
                tiles = []
                for a in range(3):
                    tap = kernels[layer][9 * a + 3 * b + c]
                    tiles.append(jnp.concatenate([tap] * (LANES // channels), axis=1))
                upper = jnp.where(in_low, tiles[1], tiles[2])
                lower = jnp.where(in_low, tiles[0], tiles[1])
                whole = jnp.concatenate([upper, lower], axis=0)
                turned = jnp.concatenate([whole, whole], axis=0).T[:planes]
                for ref, value, bb, cc in ((forward, whole, b, c), (backward, turned, 2 - b, 2 - c)):
                    base, lanes = layer * 2 * planes, pl.ds((bb * 3 + cc) * LANES, LANES)
                    high, low = split(value)
                    ref[pl.ds(base, planes), lanes] = high
                    ref[pl.ds(base + planes, planes), lanes] = low


def conv(weights, layer, window):
    planes = weights.shape[0] // (LAYERS * 2)
    kernel = weights[pl.ds(layer * 2 * planes, 2 * planes), :]
    total = lax.dot_general(kernel, window, NN, preferred_element_type=F32)
    return total[:planes] + total[planes:]


def conv_rows(weights, layer, source, low, high):
    out = {}
    for e in range(low, high, 4):
        count = min(4, high - e)
        window = [source[:, pl.ds((e + b - 1) * LANES, count * LANES)] for b in range(3)]
        value = conv(weights, layer, jnp.concatenate(window, axis=0))
        for k in range(count):
            out[e + k] = value[:, k * LANES : (k + 1) * LANES]
    return out


def store_split(target, c, lanes, value):
    planes = value.shape[0]
    high, low = split(value)
    target[pl.ds(c * LANES, planes), lanes] = high
    target[pl.ds(c * LANES + planes, planes), lanes] = low


def shift_rows(main, side, into, edges=None):
    lane = lane_index(side.shape[0])
    for e, value in main:
        base, start = e * SIDE, e * LANES
        if not isinstance(e, int):
            start = pl.multiple_of(start, LANES)
        ends = roll(side, -base)
        down = roll(jnp.where(lane == LANES - 1, ends, value), 1)
        up = roll(jnp.where(lane == 0, ends, value), -1)
        for c, shifted in enumerate((down, value, up)):
            store_split(into, c, pl.ds(start, LANES), shifted)
        if edges is not None:
            edges = jnp.where((lane == base) | (lane == base - 1), roll(value, base), edges)
    return edges


def shift_side(side, edges, into):
    place = lax.rem(lane_index(side.shape[0]), SIDE)
    ahead = roll(jnp.where(place == 0, edges, side), -1)
    behind = roll(jnp.where(place == SIDE - 1, edges, side), 1)
    for c, shifted in enumerate((behind, side, ahead)):
        store_split(into, c, pl.ds(0, LANES), shifted)


def side_strips(got, y_odd):
    zero = jnp.zeros_like(got[0])
    got = (got + [zero])[:2]
    from_right = jnp.where(y_odd, got[1], got[0])
    from_left = jnp.where(y_odd, got[0], got[1])
    return jnp.where(lax.rem(lane_index(zero.shape[0]), SIDE) >= HALO, from_right, from_left)


def field_side(f, rows, before, own, after):
    lane = lane_index(own.shape[0])
    span, lead = rows * SIDE, HALO * SIDE - HALO
    before = roll(before, lead - span - f * span)
    after = roll(after, lead + span - f * span)
    side = jnp.where(lane < lead + span, roll(own, lead - f * span), after)
    side = jnp.where(lane < lead, before, side)
    return jnp.where(lane < lead + 2 * span, side, 0.0)


INPUTS = (0, 2, 3)


def early_kernel(depth, rows, *refs):
    local, sibling, *strips = refs[: -2 * LAYERS]
    shifted, edges = refs[-2 * LAYERS : -LAYERS], refs[-LAYERS:]
    planes = local.shape[0] // (4 * rows)
    odd = lax.rem(lax.axis_index("gx"), 2)
    y_odd = lax.rem(lax.axis_index("gy"), 2) == 1
    own, inner = (side_strips([v[pl.ds(k * planes, planes), :] for v in strips], y_odd) for k in range(2))
    for layer, f in enumerate(INPUTS):
        width = WIDTHS[f]
        side = field_side(f, rows, inner, own, inner)
        main = [(HALO + r, slab_at(local, f, depth, rows, r)) for r in range(rows)]
        for j in range(width):
            e = odd * (HALO - width) + (1 - odd) * (HALO + rows) + j
            main.append((e, slab_at(sibling, f, depth, rows, (rows - width) * odd + j)))
        zero = jnp.zeros((planes, LANES), F32)
        edges[layer][...] = shift_rows(main, side, shifted[layer], zero)


def conv_side(weights, layer, shifted):
    planes = weights.shape[0] // (LAYERS * 2)
    parts = []
    for b in range(3):
        kernel = weights[pl.ds(layer * 2 * planes, 2 * planes), pl.ds(b * 3 * LANES, 3 * LANES)]
        part = lax.dot_general(kernel, shifted[...], NN, preferred_element_type=F32)
        parts.append(roll(part[:planes] + part[planes:], -(b - 1) * SIDE))
    return parts[0] + parts[1] + parts[2]


def layers_kernel(depth, rows, channels, gy_rounds, factor, *refs):
    refs = list(refs)
    take = lambda count: [refs.pop(0) for _ in range(count)]
    local, sibling, outer = take(3)
    strips, corners = take(gy_rounds), take(gy_rounds)
    forward, backward = take(2)
    early_edges = take(LAYERS)
    take(LAYERS)
    h_out, keep, send = take(3)
    shifted = take(LAYERS)
    xside, hs, hside, gsum = refs
    planes = depth * channels
    gx, gy = lax.axis_index("gx"), lax.axis_index("gy")
    gx_size, gy_size = lax.axis_size("gx"), lax.axis_size("gy")
    x_odd, y_odd = lax.rem(gx, 2) == 1, lax.rem(gy, 2) == 1
    odd = lax.rem(gx, 2)
    ended = (gx == 0) | (gx == gx_size - 1)
    lane = lane_index(planes)

    own, inner = (side_strips([v[pl.ds(k * planes, planes), :] for v in strips], y_odd) for k in range(2))
    corner = jnp.where(ended, 0.0, side_strips([v[...] for v in corners], y_odd))
    before, after = jnp.where(x_odd, inner, corner), jnp.where(x_odd, corner, inner)

    def outer_row(f, j):
        value = outer[pl.ds((STARTS[f] + j) * planes, planes), :]
        return jnp.where(ended, 0.0, value)

    def cotangent_rows():
        f, main = 1, {}
        width = WIDTHS[f]
        for j in range(width):
            a = slab_at(sibling, f, depth, rows, (rows - width) * odd + j)
            b = outer_row(f, j)
            main[HALO - width + j] = jnp.where(x_odd, a, b)
            main[HALO + rows + j] = jnp.where(x_odd, b, a)
        for r in range(rows):
            main[HALO + r] = slab_at(local, f, depth, rows, r)
        return main

    side_row = (lane + HALO) // SIDE
    right = lax.rem(lane + HALO, SIDE) >= HALO
    row_low = jnp.where(gx > 0, 0, HALO)
    row_high = jnp.where(gx < gx_size - 1, 2 * HALO + rows, HALO + rows)
    col_ok = jnp.where(right, (gy < gy_size - 1).astype(jnp.int32), (gy > 0).astype(jnp.int32))
    side_ok = (side_row >= row_low) & (side_row < row_high) & (col_ok > 0)

    padding = gsum.shape[0] - LAYERS * 7 * channels
    if padding:
        gsum[pl.ds(LAYERS * 7 * channels, padding), :] = jnp.zeros((padding, LANES), F32)
    grad_main, grad_side = cotangent_rows(), field_side(1, rows, before, own, after)
    half = lane_index(channels)
    for layer in range(LAYERS):
        f, xs = INPUTS[layer], shifted[layer]
        x_side = field_side(f, rows, before, own, after)
        x_main = []
        for j in range(WIDTHS[f]):
            e = (1 - odd) * (HALO - WIDTHS[f]) + odd * (HALO + rows) + j
            x_main.append((e, outer_row(f, j)))
        shift_side(x_side, shift_rows(x_main, x_side, xs, early_edges[layer][...]), xside)
        h_width = LAYERS - 1 - layer
        low, high = HALO - h_width, HALO + rows + h_width
        pre = conv_rows(forward, layer, xs, low, high)
        h_main = {}
        for e in range(low, high):
            value = grad_main[e] * gelu_slope(pre[e])
            if e < HALO:
                value = jnp.where(gx > 0, value, 0.0)
            if e >= HALO + rows:
                value = jnp.where(gx < gx_size - 1, value, 0.0)
            h_main[e] = value
        h_side = jnp.where(side_ok, grad_side * gelu_slope(conv_side(forward, layer, xside)), 0.0)
        if h_width:
            edges = shift_rows(h_main.items(), h_side, hs, jnp.zeros((planes, LANES), F32))
            shift_side(h_side, edges, hside)
            center = hs[pl.ds(LANES, 2 * planes), pl.ds(HALO * LANES, rows * LANES)]
        else:
            parts = [split(h_main[HALO + r]) for r in range(rows)]
            center = [jnp.concatenate([part[k] for part in parts], axis=1) for k in range(2)]
            center = jnp.concatenate(center, axis=0)
        blocks = []
        for m in range(9):
            at = pl.ds((HALO + m // 3 - 1) * LANES, rows * LANES)
            base = m % 3 * LANES
            parts = [xs[pl.ds(base + k * planes, planes), at] for k in range(2)]
            blocks.append(jnp.concatenate(parts, axis=1))
        window = jnp.concatenate(blocks + blocks[-1:], axis=0)
        center = jnp.concatenate([center, center], axis=1)
        product = lax.dot_general(center, window, NT, preferred_element_type=F32)
        product = (product[:planes] + product[planes:]) * factor
        first = lax.rem(half // channels, 2) == 0
        mixed, summed = [], []
        for t in range(5):
            part = product[:, t * LANES : (t + 1) * LANES]
            upper, lower = part[:channels], part[channels:]
            mixed.append(jnp.where(first, lower, upper))
            summed.append(upper + roll(lower, -channels))
        tiles = mixed[:4] + [jnp.where(half < planes, mixed[4], summed[4])]
        for t in (0, 2):
            tiles.append(jnp.where(first, summed[t], roll(summed[t + 1], channels)))
        for m, tile in enumerate(tiles):
            gsum[pl.ds((layer * 7 + m) * channels, channels), :] = tile

        if h_width:
            g_width = h_width - 1
            grad_main = conv_rows(backward, layer, hs, HALO - g_width, HALO + rows + g_width)
            grad_side = conv_side(backward, layer, hside)

    for r in range(rows):
        h_out[pl.ds(r * planes, planes), :] = h_main[HALO + r]
    h_out[pl.ds(rows * planes, planes), :] = h_side
    head, tail = h_main[HALO], h_main[HALO + rows - 1]
    base = keep.shape[0]
    send[pl.ds(base, planes), :] = jnp.where(x_odd, head, tail)
    send[pl.ds(base + planes, planes), :] = jnp.where(x_odd, tail, head)
    send[pl.ds(base + 2 * planes, planes), :] = h_side
    size = keep.shape[0] // 4
    core, quad = quad_place(gx, gy)
    for k in range(4):
        piece = lax.bitwise_xor(quad, k) * size
        at = pl.ds(k * size, size)
        keep[at, :] = gsum[pl.ds(pl.multiple_of(core * 4 * size + piece, 8), size), :]
        send[at, :] = gsum[pl.ds(pl.multiple_of((1 - core) * 4 * size + piece, 8), size), :]


def quad_place(gx, gy):
    return lax.rem(gx, 2), lax.rem(gy, 2) + 2 * lax.rem(gx // 2, 2)


def grad_kernel(depth, rows, channels, own, swapped, ringed, backward, grad_out, hs):
    planes = depth * channels
    gx, gx_size = lax.axis_index("gx"), lax.axis_size("gx")
    x_odd, ended = lax.rem(gx, 2) == 1, (gx == 0) | (gx == gx_size - 1)
    lane = lane_index(planes)
    span = rows * SIDE
    inner, inner_side = swapped[pl.ds(0, planes), :], swapped[pl.ds(2 * planes, planes), :]
    outer = jnp.where(ended, 0.0, ringed[pl.ds(0, planes), :])
    outer_side = jnp.where(ended, 0.0, ringed[pl.ds(planes, planes), :])
    main = {HALO + r: own[pl.ds(r * planes, planes), :] for r in range(rows)}
    main[HALO - 1] = jnp.where(x_odd, inner, outer)
    main[HALO + rows] = jnp.where(x_odd, outer, inner)
    before = roll(jnp.where(x_odd, inner_side, outer_side), -span)
    after = roll(jnp.where(x_odd, outer_side, inner_side), span)
    side = own[pl.ds(rows * planes, planes), :]
    lead = HALO * SIDE - HALO
    side = jnp.where(lane < lead, before, jnp.where(lane < lead + span, side, after))
    shift_rows(main.items(), side, hs)
    grad_main = conv_rows(backward, LAYERS - 1, hs, HALO, HALO + rows)
    for r in range(rows):
        for z in range(depth):
            at = pl.ds(z * rows + r, channels, stride=depth * rows)
            grad_out[at, :] = grad_main[HALO + r][z * channels : (z + 1) * channels]


def unpack_kernel(channels, mine, other, *refs):
    outs, whole = refs[:LAYERS], refs[LAYERS]
    size = mine.shape[0] // 4
    core, quad = quad_place(lax.axis_index("gx"), lax.axis_index("gy"))
    for k in range(4):
        piece = lax.bitwise_xor(quad, k) * size
        at = pl.ds(k * size, size)
        whole[pl.ds(pl.multiple_of(core * 4 * size + piece, 8), size), :] = mine[at, :]
        whole[pl.ds(pl.multiple_of((1 - core) * 4 * size + piece, 8), size), :] = other[at, :]
    places = [[(s % 2 * 2, 2 * t + s // 2) for s in range(4)] for t in range(4)]
    places.append([(0, 8), (2, 8), (1, 8)])
    places += [[(1, t + k) for k in (0, 2, 1, 3)] for t in (0, 4)]
    for layer in range(LAYERS):
        for t, blocks in enumerate(places):
            tile = whole[pl.ds((layer * 7 + t) * channels, channels), :]
            for s, (a, m) in enumerate(blocks):
                outs[layer][9 * a + m] = roll(tile, -s * channels)[:, :channels]


def pair_rounds(size):
    rounds = []
    for start in range(2):
        pairs = [(i, i + 1) for i in range(start, size - 1, 2)]
        if pairs:
            rounds.append(pairs + [(j, i) for i, j in pairs])
    return rounds


def reduce_halves(keep, send, beside, gx_size, gy_size):
    axes = ("gx", "gy")
    total = gx_size * gy_size

    def swap(value, bits):
        return lax.ppermute(value, axes, [(i, i ^ bits) for i in range(total)])

    core, quad = gy_size, (1, 2 * gy_size, 2 * gy_size + 1)
    got = swap(send, core)
    count = keep.shape[0]
    value, beside = keep + got[:count], beside(got[count:])
    size = value.shape[0] // 4
    pieces = [value[k * size : (k + 1) * size] for k in range(4)]
    got = [swap(pieces[k + 1], quad[k]) for k in range(3)]
    value = (pieces[0] + got[0]) + (got[1] + got[2])
    bits = [gy_size << k for k in range(2, gx_size.bit_length() - 1)]
    bits += [1 << k for k in range(1, gy_size.bit_length() - 1)]
    while bits:
        low, *high = bits[:2]
        if high:
            got = [swap(value, b) for b in (low, high[0], low | high[0])]
            value = (value + got[0]) + (got[1] + got[2])
        else:
            value = value + swap(value, low)
        bits = bits[2:]
    value, beside = lax.optimization_barrier((value, beside))
    value = jnp.concatenate([value] + [swap(value, b) for b in quad])
    return value, swap(value, core), beside


def per_device(input_one, input_two, input_three, cotangent, kernel_one, kernel_two, kernel_three):
    channels, depth, rows, cols = input_one.shape
    gx_size, gy_size = lax.axis_size("gx"), lax.axis_size("gy")
    planes = channels * depth
    factor = 1.0 / math.sqrt(depth * rows * cols * gx_size * gy_size)
    fields = [v.reshape(planes * rows, cols) for v in (input_three, cotangent, input_two, input_one)]
    shape = jax.ShapeDtypeStruct

    kernels = [kernel_three, kernel_two, kernel_one]
    size = planes * rows
    local = pl.pallas_call(
        fetch_fields,
        out_shape=pltpu.VMEM((4 * size, cols), F32),
        in_specs=[pl.BlockSpec(memory_space=pltpu.HBM)] * 4,
        out_specs=vmem(1)[0],
        scratch_shapes=[pltpu.SemaphoreType.DMA((4,))],
        compiler_params=room(8),
        name="fetch",
    )(*(far(v) for v in fields))

    sibling = lax.ppermute(local, "gx", [(i, i ^ 1) for i in range(gx_size)])
    kernels = pl.pallas_call(
        fetch_kernels,
        out_shape=[pltpu.VMEM(v.shape, F32) for v in kernels],
        in_specs=[pl.BlockSpec(memory_space=pltpu.HBM)] * LAYERS,
        out_specs=vmem(LAYERS),
        scratch_shapes=[pltpu.SemaphoreType.DMA((LAYERS,))],
        compiler_params=room(8),
        cost_estimate=pl.CostEstimate(flops=0, bytes_accessed=4_000_000, transcendentals=0),
        name="fetch_kernels",
    )(*(far(v) for v in kernels))
    sibling, *kernels = lax.optimization_barrier((sibling, *kernels))
    across = [(i, i - 2) if i % 2 else (i, i + 2) for i in range(gx_size)]
    across = [(i, j) if 0 <= j < gx_size else (i, i ^ 1) for i, j in across]
    y_rounds = pair_rounds(gy_size)
    outer = pl.pallas_call(
        functools.partial(pack_rows, depth, rows),
        out_shape=pltpu.VMEM((SLABS * planes, cols), F32),
        in_specs=vmem(1),
        out_specs=vmem(1)[0],
        compiler_params=room(8),
        name="pack_rows",
    )(near(sibling))
    strips, strip = pl.pallas_call(
        functools.partial(pack_strips, depth, rows),
        out_shape=[pltpu.VMEM((2 * planes, cols), F32), pltpu.VMEM((planes, cols), F32)],
        in_specs=vmem(2),
        out_specs=vmem(2),
        compiler_params=room(8),
        cost_estimate=pl.CostEstimate(flops=5_000_000, bytes_accessed=2_000_000, transcendentals=0),
        name="pack_strips",
    )(near(local), near(sibling))

    strips, *kernels = lax.optimization_barrier((strips, *kernels))
    weight_shape = pltpu.VMEM((LAYERS * 2 * planes, 9 * LANES), BF16)
    forward, backward = pl.pallas_call(
        functools.partial(weight_kernel, channels, depth),
        out_shape=[weight_shape, weight_shape],
        in_specs=vmem(LAYERS),
        out_specs=vmem(2),
        cost_estimate=pl.CostEstimate(flops=20_000_000, bytes_accessed=4_000_000, transcendentals=0),
        compiler_params=room(12),
        name="weights",
    )(*(near(v) for v in kernels))

    def diagonal(x_pairs, y_pairs):
        return [(i * gy_size + k, j * gy_size + m) for i, j in x_pairs for k, m in y_pairs]

    outer = lax.ppermute(outer, "gx", across)
    corners = [lax.ppermute(strip, ("gx", "gy"), diagonal(across, pairs)) for pairs in y_rounds]
    strips = [lax.ppermute(strips, "gy", pairs) for pairs in y_rounds]

    tiles = -(-LAYERS * 7 * channels // 64) * 64
    span = (2 * HALO + rows) * LANES
    shifted, shifted_side = pltpu.VMEM((3 * LANES, span), BF16), pltpu.VMEM((3 * LANES, LANES), BF16)
    early = pl.pallas_call(
        functools.partial(early_kernel, depth, rows),
        out_shape=[shifted] * LAYERS + [pltpu.VMEM((planes, LANES), F32)] * LAYERS,
        in_specs=vmem(2 + len(strips)),
        out_specs=vmem(2 * LAYERS),
        compiler_params=room(12),
        cost_estimate=pl.CostEstimate(flops=20_000_000, bytes_accessed=6_000_000, transcendentals=0),
        name="early",
    )(*(near(v) for v in (local, sibling, *strips)))
    operands = [local, sibling, outer, *strips, *corners, forward, backward, *early[LAYERS:]]
    count = len(operands)
    h_own, keep, send, *_ = pl.pallas_call(
        functools.partial(layers_kernel, depth, rows, channels, len(y_rounds), factor),
        out_shape=[
            pltpu.VMEM(((rows + 1) * planes, LANES), F32),
            pltpu.VMEM((tiles // 2, LANES), F32),
            pltpu.VMEM((tiles // 2 + 3 * planes, LANES), F32),
        ]
        + [shifted] * LAYERS,
        in_specs=vmem(count + LAYERS),
        out_specs=vmem(3 + LAYERS),
        input_output_aliases={count + k: 3 + k for k in range(LAYERS)},
        scratch_shapes=[shifted_side, shifted, shifted_side, pltpu.VMEM((tiles, LANES), F32)],
        compiler_params=room(16),
        name="layers",
    )(*(near(v) for v in operands + list(early[:LAYERS])))

    def input_gradient(swapped):
        ringed = lax.ppermute(swapped[planes:], "gx", across)
        return pl.pallas_call(
            functools.partial(grad_kernel, depth, rows, channels),
            out_shape=shape((planes * rows, cols), F32),
            in_specs=vmem(4),
            out_specs=vmem(1)[0],
            scratch_shapes=[shifted],
            compiler_params=room(8),
            cost_estimate=pl.CostEstimate(flops=600_000_000, bytes_accessed=1_000_000, transcendentals=0),
            name="grad_input",
        )(near(h_own), near(swapped), near(ringed), near(backward))

    mine, other, grad = reduce_halves(keep, send, input_gradient, gx_size, gy_size)
    results = pl.pallas_call(
        functools.partial(unpack_kernel, channels),
        out_shape=[shape(kernel_one.shape, F32)] * LAYERS,
        in_specs=vmem(2),
        out_specs=vmem(LAYERS),
        scratch_shapes=[pltpu.VMEM((tiles, LANES), F32)],
        compiler_params=room(8),
        name="unpack",
    )(near(mine), near(other))
    return (grad.reshape(input_one.shape), results[2], results[1], results[0])


def solution(mesh):
    placed = (
        P(None, None, "gx", "gy"),
        P(None, None, "gx", "gy"),
        P(None, None, "gx", "gy"),
        P(None, None, "gx", "gy"),
        P(),
        P(),
        P(),
    )
    return jax.shard_map(
        per_device,
        mesh=mesh,
        in_specs=placed,
        out_specs=(P(None, None, "gx", "gy"), P(), P(), P()),
        check_vma=False,
    )
```
